256 devices in a mesh: segment: 16 (over x, y), mp: 16 (over z, core).
Axes of the slice: x: 4, y: 4, z: 8, core: 2. Of those that a mesh axis runs over, the one named last changes fastest.
Arguments:
- noise_init: float32 [8192, 64], P('segment'), may hold values from -6 to 6
- step_noise: float32 [4, 8192, 64], P(None, 'segment'), may hold values from -6 to 6
- assign: int32 [128], P('segment'), may hold values from 0 to 31
- slot_map: int32 [128], replicated, may hold values from 0 to 255, as said below
- prompt_embed: bfloat16 [32, 1536], P('segment', 'mp'), may hold values from -6 to 6
- time_vec: bfloat16 [1536], P('mp'), may hold values from -6 to 6
- w_in: bfloat16 [64, 1536], P('segment', 'mp'), may hold values from -0.75 to 0.75
- ln_gain: bfloat16 [1536], P('mp'), may hold values from 0.099609375 to 1.8984375
- w_up: bfloat16 [1536, 6144], P('segment', 'mp'), may hold values from -0.15625 to 0.15625
- w_down: bfloat16 [6144, 1536], P('mp', 'segment'), may hold values from -0.109375 to 0.109375
- w_out: bfloat16 [1536, 64], P('mp', 'segment'), may hold values from -0.15625 to 0.15625
- conv_in_w: bfloat16 [3, 3, 16, 512], replicated, may hold values from -0.5 to 0.5
- gn_gain: float32 [512], replicated, may hold values from 0.1 to 1.9
- conv_mid_w: bfloat16 [3, 3, 512, 512], replicated, may hold values from -0.09375 to 0.09375
Outputs:
- latents: float32 [8192, 64], P('segment')
- decoded: bfloat16 [256, 2, 128, 512], P('segment', None, 'mp')
The draws below stay inside these ranges and needn't reach their ends.
Inputs may be any that keep to these rules, and one draw needn't show every extreme that they name: `slot_map`: different samples have different slots. Decoder section d owns slots d * 16 to (d + 1) * 16 - 1; in every draw some section has all of its 16 slots filled, and slots 0 and 255 are used.
All inputs are finite; a program needn't handle non-finite values.
Results may differ from the reference program's by a relative error of at most 0.015.
Values may be sent and summed in bfloat16 or wider, within the bound.
A program may use at most 64 MiB of HBM per device.

```python
import jax
import jax.numpy as jnp
from jax import lax

D = 1536
FF = 6144
LAT_CH = 16
VC = 512
GROUPS = 32
LCOLS = 128
STEPS = 4
PCH = 64
TOK_SAMPLE = 64
DSLOT = 16
SAMPLES = 128
TOKENS = 8192
SLOTS = 256
PROMPTS = 32
N_MP = 16


def draw_slot_map(key, part):
    section_key = jax.random.fold_in(key, 101)
    order_key = jax.random.fold_in(key, 202)
    sample_key = jax.random.fold_in(key, 303)
    sections = SLOTS // DSLOT
    chosen_section = jax.random.randint(section_key, (), 0, sections).astype(jnp.int32)
    shuffled = jax.random.permutation(order_key, SLOTS).astype(jnp.int32)
    positions = jnp.arange(SLOTS, dtype=jnp.int32)
    forced = (positions // DSLOT == chosen_section) | (positions == 0) | (positions == SLOTS - 1)
    scores = shuffled - SLOTS * forced.astype(jnp.int32)
    ordering = jnp.argsort(scores, stable=True).astype(jnp.int32)
    chosen = ordering[:SAMPLES]
    mixing = jax.random.permutation(sample_key, SAMPLES).astype(jnp.int32)
    return chosen[mixing].astype(jnp.int32)


def plant(drawn, key, smallest, largest):
    spot = [jax.random.randint(jax.random.fold_in(key, axis), (), 0, length) for axis, length in enumerate(drawn.shape)]
    longest = drawn.shape.index(max(drawn.shape))
    beside = spot[:longest] + [(spot[longest] + 1) % drawn.shape[longest]] + spot[longest + 1:]
    return drawn.at[tuple(spot)].set(smallest).at[tuple(beside)].set(largest)


def with_spikes(values, rng, source, target, shards_of, factor):
    def block_of(position):
        return (jnp.arange(values.shape[position]) // (values.shape[position] // shards_of)).reshape((-1,) + (1,) * (values.ndim - 1 - position))

    first = jax.random.permutation(rng, shards_of)[block_of(target)]
    other_side = (block_of(target) + shards_of // 2) % shards_of
    return jnp.where((block_of(source) == first) | (block_of(source) == other_side), factor * values, values)


def block_scale(own_key, shape, cuts, smallest, largest):
    factor_of, own = 1.0, jax.random.fold_in(own_key, 6)
    for dim, blocks in cuts:
        steps = jnp.exp(jax.random.uniform(jax.random.fold_in(own, dim), (blocks,), jnp.float32, smallest / len(cuts), largest / len(cuts)))
        factor_of = factor_of * jnp.repeat(steps, shape[dim] // blocks).reshape([-1 if axis == dim else 1 for axis in range(len(shape))])
    return factor_of


def scatter_about(rng, dims, scale, reach, cuts=(), kind=jnp.bfloat16):
    gain = block_scale(rng, dims, cuts, -0.22, 0.18) if cuts else 1.0
    array = jax.random.normal(rng, dims, jnp.float32) * scale * gain
    return jnp.minimum(jnp.maximum(array, -reach), reach).astype(kind)


def heavy_noise(own_key, extent, deviation, limit, cuts, heavy, kind=jnp.bfloat16):
    array = deviation * jax.random.normal(own_key, extent, jnp.float32)
    if cuts:
        array = array * block_scale(own_key, extent, cuts, -0.22, 0.18)
    return jnp.clip(with_spikes(array, jax.random.fold_in(own_key, 3), *heavy), -limit, limit).astype(kind)


def setup_inputs(seed: int = 0) -> dict:
    seeds = jax.random.split(jax.random.key(seed), 15)
    return {
        "noise_init": scatter_about(seeds[0], (TOKENS, PCH), 1.0, 6.0, ((0, 16),), jnp.float32),
        "step_noise": scatter_about(seeds[1], (STEPS, TOKENS, PCH), 1.0, 6.0, ((1, 16),), jnp.float32),
        "assign": plant(jax.random.randint(seeds[2], (SAMPLES,), 0, PROMPTS), jax.random.fold_in(seeds[2], 1), 0, PROMPTS - 1).astype(jnp.int32),
        "slot_map": draw_slot_map(jax.random.fold_in(seeds[14], 71), 0),
        "prompt_embed": scatter_about(seeds[4], (PROMPTS, D), 1.0, 6.0, ((0, 16), (1, 16))),
        "time_vec": scatter_about(seeds[5], (D,), 1.0, 6.0, ((0, 16),)),
        "w_in": scatter_about(seeds[6], (PCH, D), PCH ** -0.5, 0.75, ((0, 16), (1, 16))),
        "ln_gain": jnp.clip(1.0 + 0.18 * jax.random.normal(seeds[7], (D,), jnp.float32), 0.099609375, 1.8984375).astype(jnp.bfloat16),
        "w_up": scatter_about(seeds[8], (D, FF), D ** -0.5, 0.15625, ((0, 16), (1, 16))),
        "w_down": heavy_noise(seeds[9], (FF, D), FF ** -0.5, 0.109375, ((0, 16), (1, 16)), (0, 1, 16, 2.0)),
        "w_out": scatter_about(seeds[10], (D, PCH), D ** -0.5, 0.15625, ((0, 16), (1, 16))),
        "conv_in_w": scatter_about(seeds[11], (3, 3, LAT_CH, VC), (9 * LAT_CH) ** -0.5, 0.5),
        "gn_gain": jnp.clip(1.0 + 0.18 * jax.random.normal(seeds[12], (VC,), jnp.float32), 0.1, 1.9),
        "conv_mid_w": scatter_about(seeds[13], (3, 3, VC, VC), (9 * VC) ** -0.5, 0.09375),
    }


NOISE_SCALE = 0.5
LATENT_SCALE = 1.0 / 1.5305
EPSILON = 1e-06

def conv_three(padded, weight, col_count):
    accumulated = jnp.zeros((2, col_count, weight.shape[3]), jnp.float32)
    for row_shift in range(3):
        for col_shift in range(3):
            window = padded[row_shift:row_shift + 2, col_shift:col_shift + col_count, :]
            accumulated = accumulated + jnp.dot(window.reshape(2 * col_count, -1), weight[row_shift, col_shift], preferred_element_type=jnp.float32).reshape(2, col_count, -1)
    return accumulated

def reference(noise_init, step_noise, assign, slot_map, prompt_embed, time_vec, w_in, ln_gain, w_up, w_down, w_out, conv_in_w, gn_gain, conv_mid_w):
    prompt_cond = jnp.repeat(prompt_embed.astype(jnp.float32)[assign], TOK_SAMPLE, axis=0)
    latent_state = noise_init
    step_size = 1.0 / STEPS
    block_width = FF // N_MP
    for step_index in range(STEPS):
        time_now = 1.0 - step_index * step_size
        hidden_in = jnp.dot(latent_state.astype(jnp.bfloat16), w_in, preferred_element_type=jnp.float32) + prompt_cond + time_now * time_vec.astype(jnp.float32)
        average = lax.optimization_barrier(jnp.mean(hidden_in, axis=-1, keepdims=True))
        centered = hidden_in - average
        variance = lax.optimization_barrier(jnp.mean(centered * centered, axis=-1, keepdims=True))
        normed = (centered * lax.rsqrt(variance + EPSILON) * ln_gain.astype(jnp.float32)).astype(jnp.bfloat16)
        act = jax.nn.gelu(jnp.dot(normed, w_up, preferred_element_type=jnp.float32), approximate=True).astype(jnp.bfloat16)
        mlp_out = jnp.zeros(hidden_in.shape, jnp.float32)
        for block_index in range(N_MP):
            partial_value = jnp.dot(act[:, block_index * block_width:(block_index + 1) * block_width], w_down[block_index * block_width:(block_index + 1) * block_width], preferred_element_type=jnp.float32)
            rounded = lax.optimization_barrier(partial_value.astype(jnp.bfloat16))
            mlp_out = mlp_out + rounded.astype(jnp.float32)
        velocity = jnp.dot((hidden_in + mlp_out).astype(jnp.bfloat16), w_out, preferred_element_type=jnp.float32)
        latent_state = latent_state - step_size * velocity + NOISE_SCALE * jnp.sqrt(step_size) * step_noise[step_index]
    latents = latent_state
    images = latent_state.reshape(SAMPLES, TOK_SAMPLE, 2, 2, LAT_CH).transpose(0, 2, 1, 3, 4).reshape(SAMPLES, 2, LCOLS, LAT_CH)
    slot_in = jnp.zeros((SLOTS, 2, LCOLS, LAT_CH), jnp.float32).at[slot_map].set(images * LATENT_SCALE)
    per_group = VC // GROUPS

    def decode_one(latent_img):
        padded = jnp.pad(latent_img.astype(jnp.bfloat16), ((1, 1), (1, 1), (0, 0)))
        conv_first = conv_three(padded, conv_in_w, LCOLS)
        grouped = conv_first.reshape(2 * LCOLS, GROUPS, per_group)
        average = lax.optimization_barrier(jnp.mean(grouped, axis=(0, 2)))
        centered = grouped - average[None, :, None]
        variance = lax.optimization_barrier(jnp.mean(centered * centered, axis=(0, 2)))
        normed = (centered * lax.rsqrt(variance + EPSILON)[None, :, None]).reshape(2, LCOLS, VC) * gn_gain
        activated = jax.nn.silu(normed).astype(jnp.bfloat16)
        padded_act = jnp.pad(activated, ((1, 1), (1, 1), (0, 0)))
        return (conv_first + conv_three(padded_act, conv_mid_w, LCOLS)).astype(jnp.bfloat16)
    decoded = lax.map(decode_one, slot_in)
    return (latents, decoded)
```

```python
import jax
import jax.numpy as jnp
from jax import lax
from jax.experimental import pallas as pl
from jax.experimental.pallas import tpu as pltpu
from jax.sharding import PartitionSpec as P

MESH = pl.DeviceIdType.MESH
F32, BF16 = jnp.float32, jnp.bfloat16
HIGH = lax.Precision.HIGHEST
D, FF, VC, GROUPS, STEPS = 1536, 6144, 512, 32, 4
EPSILON = 1e-6
LATENT_SCALE = 1.0 / 1.5305
STEP = 1.0 / STEPS
NOISE_GAIN = 0.5 * STEP**0.5
TIME_ROW, ONES_ROW, GAIN_ROW = 160, 161, 162
Z_ORDER = (1, 7, 2, 6, 3, 5, 4)


def dot(a, b, **kw):
    return jnp.dot(a, b, preferred_element_type=F32, **kw)


def dot_t(a, b):
    return lax.dot_general(a, b, (((1,), (1,)), ((), ())), preferred_element_type=F32)


def iota(shape, dim):
    return lax.broadcasted_iota(jnp.int32, shape, dim)


def onehot(mask):
    return jnp.where(mask, 1.0, 0.0).astype(BF16)


def split(value):
    high = value.astype(BF16)
    return high, (value - high.astype(F32)).astype(BF16)


def kernel(
    assign, slot_map, noise0, noise_k, prompt, time_vec, w_in, gain, w_up, w_down, w_out, conv_in, gn_gain, conv_mid,
    lat_ref, dec_ref,
    piece, tables, gram, part, parts, chunks, gy_own, gy_z, gy_all, vel_out, vel_in, state,
    tile_out, tile_z, tile_pack, tiles, lat_out, lat_in, noise_a, noise_b, w_mid, w_tok, act0, act1,
    in_sem, send_p, recv_p, send_r, recv_r, send_z, recv_z, send_g, recv_g, send_c, recv_c, send_h, recv_h,
    send_v, recv_v, send_t, recv_t, send_u, recv_u, send_l, recv_l,
):
    s, m = lax.axis_index("segment"), lax.axis_index("mp")
    z, c = lax.div(m, 2), lax.rem(m, 2)
    on_diagonal = m == s

    def remote(src, dst, ssem, rsem, device):
        return pltpu.make_async_remote_copy(
            src_ref=src, dst_ref=dst, send_sem=ssem, recv_sem=rsem, device_id=device, device_id_type=MESH
        )

    def plane(i):
        return lax.rem(s + i, 16), m

    def along_z(i):
        return s, lax.rem(z + i, 8) * 2 + c

    other_core = (s, m + 1 - 2 * c)

    def drain(ref, sem):
        pltpu.make_async_copy(ref, ref, sem).wait()

    barrier = pltpu.get_barrier_semaphore()

    def greet(device):
        pl.semaphore_signal(barrier, inc=1, device_id=device, device_id_type=MESH)

    @pl.loop(0, 16)
    def _(i):
        @pl.when(jnp.logical_not(jnp.logical_and(on_diagonal, i == s)))
        def _():
            greet((i, s))

    @pl.loop(1, 16)
    def _(i):
        greet(plane(i))

    @pl.loop(1, 8)
    def _(i):
        greet(along_z(i))

    greet(other_core)

    rows = pl.ds(pl.multiple_of(z * 64, 64), 64)
    in_noise = pltpu.make_async_copy(noise0.at[rows], noise_a, in_sem.at[0])
    in_steps = pltpu.make_async_copy(noise_k.at[:, rows], noise_b, in_sem.at[1])
    in_mid = pltpu.make_async_copy(conv_mid, w_mid, in_sem.at[2])
    in_noise.start()
    in_steps.start()
    in_mid.start()

    first = jnp.where(s == 0, 1.0, 0.0)
    turned = dot_t(onehot(iota((4, 4), 0) == iota((4, 4), 1)), w_out[...])
    block = jnp.concatenate(
        [
            w_in[...].astype(F32),
            prompt[...].astype(F32),
            time_vec[...].astype(F32).reshape(1, 96) * first,
            jnp.ones((1, 96), F32),
            turned,
            gain[...].astype(F32).reshape(1, 96),
            jnp.zeros((3, 96), F32),
        ],
        axis=0,
    )
    piece[...] = jnp.concatenate([block, jnp.zeros((16, 32), F32)], axis=1).astype(BF16)

    @pl.when(on_diagonal)
    def _():
        tables[s] = piece[...]

    pl.semaphore_wait(barrier, 39 - jnp.where(on_diagonal, 1, 0))

    def to_features(i):
        return remote(piece, tables.at[s], send_p, recv_p, (m, i))

    @pl.loop(0, 16)
    def _(i):
        @pl.when(jnp.logical_not(jnp.logical_and(on_diagonal, i == m)))
        def _():
            to_features(i).start()

    w_tok[...] = jnp.zeros(w_tok.shape, BF16)
    for row in range(2):
        for col in range(2):
            for src_row in range(2):
                for tap in range(3):
                    offset = col + tap - 1 + 2
                    to = (offset // 2) * 64 + (2 * src_row + offset % 2) * 16
                    at = (2 * row + col) * VC
                    w_tok[to : to + 16, at : at + VC] = conv_in[src_row - row + 1, tap]

    @pl.when(on_diagonal)
    def _():
        drain(tables.at[pl.ds(0, 15)], recv_p)

    @pl.when(jnp.logical_not(on_diagonal))
    def _():
        drain(tables, recv_p)

    want = iota((256, 256), 0)
    have = iota((256, 256), 1)
    prompt_row, out_row = want - 64, want - 96
    source = jnp.where(
        want < 64,
        (want >> 2) * 16 + (want & 3),
        jnp.where(
            want < 96,
            (prompt_row >> 1) * 16 + 4 + (prompt_row & 1),
            jnp.where(
                want < 160,
                (out_row >> 2) * 16 + 8 + (out_row & 3),
                jnp.where(want == TIME_ROW, 6, jnp.where(want == ONES_ROW, 7, jnp.where(want == GAIN_ROW, 12, -1))),
            ),
        ),
    )
    table = dot(onehot(source == have), tables[...].reshape(256, 128))
    table16 = table.astype(BF16)
    scaled_high, scaled_low = split(table * table[GAIN_ROW : GAIN_ROW + 1])
    up_part = dot(scaled_high[:, :96], w_up[...]) + dot(scaled_low[:, :96], w_up[...])
    down_part = dot_t(table16[96:160, :96], w_down[...])
    gram[...] = dot_t(table16, table16)
    for third in range(3):
        lanes = slice(128 * third, 128 * third + 128)
        for group in range(10):
            number = third * 10 + group
            to = (number % 2) * 16
            if group < 6:
                part[number // 2, to : to + 16] = up_part[16 * group : 16 * group + 16, lanes]
            else:
                part[number // 2, to : to + 16] = down_part[16 * group - 96 : 16 * group - 80, lanes]
    part[15, 0:32] = jnp.zeros((32, 128), F32)
    for third in range(3):
        lanes = slice(128 * third, 128 * third + 128)
        part[15, third : third + 1] = up_part[TIME_ROW : TIME_ROW + 1, lanes]
    gain_up = jnp.concatenate(
        [up_part[ONES_ROW : ONES_ROW + 1, 128 * third : 128 * third + 128] for third in range(3)], axis=0
    )
    sums = gram[ONES_ROW : ONES_ROW + 1]
    for owner in range(16):
        first_row = 8 * owner + (64 if owner >= 12 else 0)
        own = gram[pl.ds(first_row + z, 1)]
        part[owner, 32:40] = jnp.concatenate(
            [sums[:, :128], sums[:, 128:], gain_up, own[:, :128], own[:, 128:], jnp.zeros((1, 128), F32)], axis=0
        )

    def to_owner(i):
        target = lax.rem(s + i, 16)
        return remote(part.at[target], parts.at[s], send_r, recv_r, (target, m))

    @pl.loop(1, 16)
    def _(i):
        to_owner(i).start()

    parts[s] = part[s]
    drain(parts.at[pl.ds(0, 15)], recv_r)

    total = parts[0]
    for source_s in range(1, 16):
        total = total + parts[source_s]
    mean = jnp.concatenate([total[32:33], total[33:34]], axis=1) / D
    gain_rows = total[34:37]
    lane16 = iota((16, 256), 1)
    row16 = iota((16, 256), 0)
    mean_time = jnp.sum(jnp.where(iota((1, 256), 1) == TIME_ROW, mean, 0.0), axis=1, keepdims=True)
    for half in range(2):
        number = 2 * s + half
        third = lax.div(number, 10)
        group = lax.rem(number, 10)
        block = total[16 * half : 16 * half + 16]
        column = jnp.sum(jnp.where(lane16 == row16 + 16 * group, mean, 0.0), axis=1, keepdims=True)
        column = jnp.where(group < 6, column, 0.0)
        row = jnp.where(third == 0, gain_rows[0:1], jnp.where(third == 1, gain_rows[1:2], gain_rows[2:3]))
        if half == 0:
            time_rows = jnp.concatenate([mean_time * gain_rows, jnp.zeros((13, 128), F32)], axis=0)
        else:
            time_rows = jnp.zeros((16, 128), F32)
        taken = jnp.where(s == 15, time_rows, column * row)
        chunks[z, s, 16 * half : 16 * half + 16] = (block - taken).astype(BF16)
    own = jnp.concatenate([total[37:38], total[38:39]], axis=1)
    own_index = 8 * s + z
    own_lane = own_index + jnp.where(own_index >= 96, 64, 0)
    lane1 = iota((1, 256), 1)
    own_mean = jnp.sum(jnp.where(lane1 == own_lane, mean, 0.0), axis=1, keepdims=True)
    is_gram = jnp.logical_or(lane1 < 96, lane1 == TIME_ROW)
    own = jnp.where(is_gram, own / D - own_mean * mean, own)
    gy_own[...] = jnp.concatenate([own[:, :128], own[:, 128:], jnp.zeros((6, 128), F32)], axis=0)
    gy_z[z] = gy_own[...]

    def chunk_z(i):
        return remote(chunks.at[z, s], chunks.at[z, s], send_z, recv_z.at[i], along_z(i))

    def gram_z(i):
        return remote(gy_own, gy_z.at[z], send_g, recv_g, along_z(i))

    for i in Z_ORDER:
        chunk_z(i).start()
        gram_z(i).start()

    def chunk_plane(i, k):
        at = lax.rem(z + 8 - i, 8)
        return remote(chunks.at[at, s], chunks.at[at, s], send_c, recv_c.at[i], plane(k))

    @pl.loop(1, 16)
    def _(k):
        chunk_plane(0, k).start()

    for n, i in enumerate(Z_ORDER):
        chunk_z(i).wait_recv()

        @pl.loop(1, 16)
        def _(k):
            chunk_plane(i, k).start()

        if n == 2:
            pass
    drain(gy_z.at[pl.ds(0, 7)], recv_g)
    gy_all[s] = jnp.concatenate(
        [jnp.concatenate([gy_z[i, 0:1] for i in range(8)], axis=0), jnp.concatenate([gy_z[i, 1:2] for i in range(8)], axis=0)],
        axis=1,
    )

    def gram_plane(k):
        return remote(gy_all.at[s], gy_all.at[s], send_h, recv_h, plane(k))

    @pl.loop(1, 16)
    def _(k):
        gram_plane(k).start()

    in_noise.wait()
    in_steps.wait()
    zero_half = jnp.zeros((64, 64), F32)
    state[...] = jnp.concatenate([noise_a[...], zero_half], axis=1)
    which = assign[z]
    drain(gy_all.at[pl.ds(0, 15)], recv_h)
    for i in (0,) + Z_ORDER:
        drain(chunks.at[0, pl.ds(0, 15)], recv_c.at[i])
    gy = gy_all[...].reshape(128, 256)
    gy_high, gy_low = split(gy)
    lane = iota((64, 128), 1)
    chosen = jnp.where(lane == 64 + which, 1.0, 0.0)

    @pl.loop(0, STEPS)
    def _(k):
        now = 1.0 - k.astype(F32) * STEP
        latent = state[...]
        rounded = latent.astype(BF16).astype(F32)
        x = rounded + chosen
        x16 = x.astype(BF16)
        x_time = (x + jnp.where(lane == 96, now, 0.0)).astype(BF16)
        mixed = dot(x_time, gy_high) + dot(x_time, gy_low)
        second = jnp.where(lane == TIME_ROW - 128, now, 0.0)
        variance = jnp.sum(mixed[:, :128] * x + mixed[:, 128:] * second, axis=1, keepdims=True)
        inv = lax.rsqrt(jnp.maximum(variance, 0.0) + EPSILON)
        skip = jnp.concatenate([mixed[:, 96:160], zero_half], axis=1)
        moved = None
        for zi in range(8):
            weights = chunks[zi].reshape(512, 128)
            up = jnp.concatenate([weights[160 * t : 160 * t + 128] for t in range(3)], axis=1)
            down = jnp.concatenate([weights[160 * t + 96 : 160 * t + 160] for t in range(3)], axis=1)
            timed = weights[480:496].astype(F32)
            bias = jnp.concatenate([timed[t : t + 1] for t in range(3)], axis=1) * now
            hidden = (dot(x16, up) + bias) * inv
            act = jax.nn.gelu(hidden, approximate=True).astype(BF16)
            product = dot_t(act, down)
            moved = product if moved is None else moved + product
        moved = jnp.concatenate([moved, zero_half], axis=1).astype(BF16)
        vel_out[k] = moved
        swap = remote(vel_out.at[k], vel_in.at[k], send_v.at[k], recv_v.at[k], other_core)
        swap.start()
        fresh = jnp.concatenate([noise_b[k], zero_half], axis=1)
        partly = latent - STEP * skip + NOISE_GAIN * fresh
        swap.wait_recv()
        state[...] = partly - STEP * (moved.astype(F32) + vel_in[k].astype(F32))

    latent = state[...][:, :64]
    image = (latent * LATENT_SCALE).astype(BF16)
    image32 = image.astype(F32)
    empty = jnp.zeros((1, 64), F32)
    before = jnp.concatenate([empty, image32[:63]], axis=0)
    after = jnp.concatenate([image32[1:], empty], axis=0)
    wide = jnp.concatenate([before, image32, after], axis=1).astype(BF16)
    conv = dot(wide, w_tok[...])
    sums4 = jnp.sum(conv, axis=0, keepdims=True)
    channel_mean = sum(sums4[:, VC * i : VC * i + VC] for i in range(4)) / 256.0
    away = conv - jnp.concatenate([channel_mean] * 4, axis=1)
    squares4 = jnp.sum(away * away, axis=0, keepdims=True)
    channel_var = sum(squares4[:, VC * i : VC * i + VC] for i in range(4)) / 256.0
    stack = jnp.concatenate(
        [channel_mean, channel_var, channel_mean * channel_mean, jnp.zeros((5, VC), F32)], axis=0
    )
    member = jnp.where((iota((VC, 128), 0) >> 4) == (iota((VC, 128), 1) & 31), 1.0, 0.0)
    grouped = dot(stack, member, precision=HIGH) / 16.0
    average = grouped[0:1]
    variance = grouped[1:2] + jnp.maximum(grouped[2:3] - average * average, 0.0)
    inv = lax.rsqrt(variance + EPSILON)
    mean_high, mean_low = split(average)
    inv_high, inv_low = split(inv)
    lane1 = iota((1, 128), 1)
    stats = jnp.where(
        lane1 < 32,
        mean_high.astype(F32),
        jnp.where(lane1 < 64, mean_low.astype(F32), jnp.where(lane1 < 96, inv_high.astype(F32), inv_low.astype(F32))),
    )
    pair, token = iota((64, 64), 0), iota((64, 64), 1)
    pairs = jnp.concatenate(
        [dot(onehot(token == 2 * pair - 1), image), dot(onehot(token == 2 * pair), image)], axis=1
    ).astype(BF16)
    row, col = iota((64, 64), 0), iota((64, 64), 1)
    place = row & 7
    wanted = jnp.logical_and(place < 3, col == 4 * (row >> 3) + 2 * c + place)
    sent = dot(onehot(wanted), pairs) + jnp.where((iota((64, 128), 0) & 7) == 3, stats, 0.0)
    tile_out[...] = sent.reshape(8, 8, 128)
    tile_z[z] = tile_out[z]

    def tile_to(i):
        to = lax.rem(z + i, 8)
        return remote(tile_out.at[to], tile_z.at[z], send_t, recv_t, (s, to * 2 + c))

    for i in Z_ORDER:
        tile_to(i).start()
    lat_out[...] = jnp.concatenate([latent[:32], latent[32:]], axis=1)
    lat_in[z] = lat_out[...]

    def latent_to(i):
        return remote(lat_out, lat_in.at[z], send_l, recv_l, along_z(i))

    for i in Z_ORDER:
        latent_to(i).start()
    drain(tile_z.at[pl.ds(0, 7)], recv_t)
    row, col = iota((32, 64), 0), iota((32, 64), 1)
    tile_pack[...] = dot(
        onehot(col == 8 * (row >> 2) + (row & 3)), tile_z[...].reshape(64, 128).astype(BF16)
    ).astype(BF16)
    tiles[s] = tile_pack[...]

    def tile_plane(k):
        return remote(tile_pack, tiles.at[s], send_u, recv_u, plane(k))

    @pl.loop(1, 16)
    def _(k):
        tile_plane(k).start()

    spread = onehot((iota((128, 512), 1) >> 2) == iota((128, 512), 0))
    slots = jnp.broadcast_to(slot_map[...].astype(F32).reshape(1, 128), (8, 128)).astype(BF16)
    slot_of = dot(slots, spread)[0:1]
    row, col = iota((64, 512), 0), iota((64, 512), 1)
    here = (16 * s + (row & 15)).astype(F32)
    pick = onehot(jnp.logical_and(slot_of == here, (col & 3) == (row >> 4)))
    in_mid.wait()
    drain(tiles.at[pl.ds(0, 15)], recv_u)
    picked = dot(pick, tiles[...].reshape(512, 128))
    tokens = jnp.concatenate(
        [picked[16 * (i // 2) : 16 * (i // 2) + 16, 64 * (i % 2) : 64 * (i % 2) + 64] for i in range(6)], axis=0
    )
    none = jnp.zeros((16, 64), F32)
    wide = jnp.concatenate(
        [jnp.concatenate([none, tokens[:80]], axis=0), tokens, jnp.concatenate([tokens[16:], none], axis=0)], axis=1
    ).astype(BF16)
    conv = dot(wide, w_tok[...])
    line, channel = iota((128, 1024), 0), iota((128, 1024), 1)
    widen = onehot(
        jnp.logical_and((line & 31) == ((channel & 511) >> 4), (line >= 64) == (channel >= 512))
    )
    wide_stats = dot(picked[48:64].astype(BF16), widen)
    average, inv = wide_stats[:, :VC], wide_stats[:, VC:]
    strength = inv * gn_gain[...].reshape(1, VC)
    left = jnp.where(m == 0, 0.0, 1.0)
    right = jnp.where(m == 15, 0.0, 1.0)
    for row, act in ((0, act0), (1, act1)):
        for at in range(10):
            token, half = (at + 1) // 2, (at + 1) % 2
            here = VC * (2 * row + half)
            shaped = (conv[16 * token : 16 * token + 16, here : here + VC] - average) * strength
            value = jax.nn.silu(shaped)
            if at == 0:
                value = value * left
            if at == 9:
                value = value * right
            act[16 * at : 16 * at + 16] = value.astype(BF16)
    order = onehot(
        iota((128, 128), 1) == (iota((128, 128), 0) & 7) * 16 + (iota((128, 128), 0) >> 3)
    )
    for row in range(2):
        total = jnp.concatenate(
            [
                conv[16 * (1 + at // 2) : 16 * (1 + at // 2) + 16, VC * (2 * row + at % 2) : VC * (2 * row + at % 2) + VC]
                for at in range(8)
            ],
            axis=0,
        )
        for tap in range(3):
            total = total + dot(act0[16 * tap : 16 * tap + 128], w_mid[1 - row, tap])
            total = total + dot(act1[16 * tap : 16 * tap + 128], w_mid[2 - row, tap])
        ordered = dot(order, total.astype(BF16)).astype(BF16)
        dec_ref[:, row] = ordered.reshape(16, 8, VC)

    drain(lat_in.at[pl.ds(0, 7)], recv_l)
    for i in range(8):
        lat_ref[64 * i : 64 * i + 32] = lat_in[i][:, :64]
        lat_ref[64 * i + 32 : 64 * i + 64] = lat_in[i][:, 64:]

    @pl.loop(0, 16)
    def _(i):
        @pl.when(jnp.logical_not(jnp.logical_and(on_diagonal, i == m)))
        def _():
            to_features(i).wait_send()

    drain(parts.at[pl.ds(0, 15)], send_r)
    drain(chunks.at[0, pl.ds(0, 7)], send_z)
    drain(gy_z.at[pl.ds(0, 7)], send_g)
    for _ in range(8):
        drain(chunks.at[0, pl.ds(0, 15)], send_c)
    drain(gy_all.at[pl.ds(0, 15)], send_h)

    @pl.loop(0, STEPS)
    def _(k):
        remote(vel_out.at[k], vel_in.at[k], send_v.at[k], recv_v.at[k], other_core).wait_send()

    drain(tile_z.at[pl.ds(0, 7)], send_t)
    drain(lat_in.at[pl.ds(0, 7)], send_l)
    drain(tiles.at[pl.ds(0, 15)], send_u)


def per_device(*args):
    vmem, anywhere, smem = (
        pl.BlockSpec(memory_space=pltpu.VMEM),
        pl.BlockSpec(memory_space=pl.ANY),
        pl.BlockSpec(memory_space=pltpu.SMEM),
    )
    noise0, noise_k, assign, slot_map, prompt, time_vec, w_in, gain, w_up, w_down, w_out, conv_in, gn_gain, conv_mid = args
    dma = pltpu.SemaphoreType.DMA
    return pl.pallas_call(
        kernel,
        out_shape=(jax.ShapeDtypeStruct((512, 64), F32), jax.ShapeDtypeStruct((16, 2, 8, VC), BF16)),
        in_specs=[smem, vmem, anywhere, anywhere] + [vmem] * 9 + [anywhere],
        out_specs=(vmem, vmem),
        scratch_shapes=[
            pltpu.VMEM((16, 128), BF16),
            pltpu.VMEM((16, 16, 128), BF16),
            pltpu.VMEM((256, 256), F32),
            pltpu.VMEM((16, 40, 128), F32),
            pltpu.VMEM((16, 40, 128), F32),
            pltpu.VMEM((8, 16, 32, 128), BF16),
            pltpu.VMEM((8, 128), F32),
            pltpu.VMEM((8, 8, 128), F32),
            pltpu.VMEM((16, 8, 256), F32),
            pltpu.VMEM((STEPS, 64, 128), BF16),
            pltpu.VMEM((STEPS, 64, 128), BF16),
            pltpu.VMEM((64, 128), F32),
            pltpu.VMEM((8, 8, 128), F32),
            pltpu.VMEM((8, 8, 128), F32),
            pltpu.VMEM((32, 128), BF16),
            pltpu.VMEM((16, 32, 128), BF16),
            pltpu.VMEM((32, 128), F32),
            pltpu.VMEM((8, 32, 128), F32),
            pltpu.VMEM((64, 64), F32),
            pltpu.VMEM((STEPS, 64, 64), F32),
            pltpu.VMEM((3, 3, VC, VC), BF16),
            pltpu.VMEM((192, 4 * VC), BF16),
            pltpu.VMEM((160, VC), BF16),
            pltpu.VMEM((160, VC), BF16),
            dma((3,)),
            dma, dma,
            dma, dma,
            dma, dma((8,)),
            dma, dma,
            dma, dma((8,)),
            dma, dma,
            dma((STEPS,)), dma((STEPS,)),
            dma, dma,
            dma, dma,
            dma, dma,
        ],
        compiler_params=pltpu.CompilerParams(collective_id=0, has_side_effects=True, vmem_limit_bytes=40 << 20),
        name="rollout",
    )(assign, slot_map, noise0, noise_k, prompt, time_vec, w_in, gain, w_up, w_down, w_out, conv_in, gn_gain, conv_mid)


def solution(mesh):
    return jax.shard_map(
        per_device,
        mesh=mesh,
        in_specs=(
            P("segment", None),
            P(None, "segment", None),
            P("segment"),
            P(),
            P("segment", "mp"),
            P("mp"),
            P("segment", "mp"),
            P("mp"),
            P("segment", "mp"),
            P("mp", "segment"),
            P("mp", "segment"),
            P(),
            P(),
            P(),
        ),
        out_specs=(P("segment", None), P("segment", None, "mp", None)),
        check_vma=False,
    )
```

```python
import jax
import jax.numpy as jnp
from jax import lax
from jax.experimental import pallas as pl
from jax.experimental.pallas import tpu as pltpu
from jax.sharding import PartitionSpec as P

MESH = pl.DeviceIdType.MESH
F32, BF16 = jnp.float32, jnp.bfloat16
HIGH = lax.Precision.HIGHEST
D, FF, VC, GROUPS, STEPS = 1536, 6144, 512, 32, 4
EPSILON = 1e-6
LATENT_SCALE = 1.0 / 1.5305
STEP = 1.0 / STEPS
NOISE_GAIN = 0.5 * STEP**0.5
TIME_ROW, ONES_ROW, GAIN_ROW = 160, 161, 162
Z_ORDER = (1, 7, 2, 6, 3, 5, 4)


def dot(a, b, **kw):
    return jnp.dot(a, b, preferred_element_type=F32, **kw)


def dot_t(a, b):
    return lax.dot_general(a, b, (((1,), (1,)), ((), ())), preferred_element_type=F32)


def iota(shape, dim):
    return lax.broadcasted_iota(jnp.int32, shape, dim)


def onehot(mask):
    return jnp.where(mask, 1.0, 0.0).astype(BF16)


def split(value):
    high = value.astype(BF16)
    return high, (value - high.astype(F32)).astype(BF16)


def kernel(
    assign_in, slot_in, noise0, noise_k, prompt_in, time_in, w_in_in, gain_in, w_up_in, w_down_in, w_out_in, conv_in_in,
    gn_in, conv_mid,
    lat_ref, dec_ref,
    assign, slot_map, prompt, time_vec, w_in, gain, w_up, w_down, w_out, conv_in, gn_gain,
    piece, tables, gram, part, parts, chunks, gy_own, gy_z, gy_all, gy_halves, vel_out, vel_in, state,
    tile_out, tile_z, tile_pack, tiles, lat_out, lat_in, noise_a, noise_b, noise_t, w_mid, w_tok, act0, act1,
    in_sem, send_p, recv_p, send_r, recv_r, send_z, recv_z, send_g, recv_g, send_c, recv_c, send_f, recv_f, send_h, recv_h, send_v, recv_v,
    send_t, recv_t, send_u, recv_u, send_l, recv_l,
):
    s, m = lax.axis_index("segment"), lax.axis_index("mp")
    z, c = lax.div(m, 2), lax.rem(m, 2)
    on_diagonal = m == s

    def remote(src, dst, ssem, rsem, device):
        return pltpu.make_async_remote_copy(
            src_ref=src, dst_ref=dst, send_sem=ssem, recv_sem=rsem, device_id=device, device_id_type=MESH
        )

    def plane(i):
        return lax.rem(s + i, 16), m

    def along_z(i):
        return s, lax.rem(z + i, 8) * 2 + c

    other_core = (s, m + 1 - 2 * c)

    def drain(ref, sem):
        pltpu.make_async_copy(ref, ref, sem).wait()

    lanes = pl.ds(pl.multiple_of(lax.div(z, 2) * 128, 128), 128)
    early = [
        pltpu.make_async_copy(src, dst, in_sem.at[3 + n])
        for n, (src, dst) in enumerate(
            [(w_in_in, w_in), (prompt_in, prompt), (time_in, time_vec), (gain_in, gain), (w_out_in, w_out)]
        )
    ]
    in_conv = pltpu.make_async_copy(conv_in_in, conv_in, in_sem.at[8])
    later = [
        pltpu.make_async_copy(src, dst, in_sem.at[9 + n])
        for n, (src, dst) in enumerate([(w_up_in, w_up), (w_down_in, w_down)])
    ]
    last = [
        pltpu.make_async_copy(src, dst, in_sem.at[11 + n])
        for n, (src, dst) in enumerate([(assign_in, assign), (slot_in, slot_map), (gn_in, gn_gain)])
    ]
    in_noise = pltpu.make_async_copy(noise0.at[:, lanes], noise_a, in_sem.at[0])
    in_steps = pltpu.make_async_copy(noise_k.at[:, :, lanes], noise_b, in_sem.at[1])
    in_mid = pltpu.make_async_copy(conv_mid, w_mid, in_sem.at[2])
    for copy in early + later + [in_conv, in_noise, in_steps] + last + [in_mid]:
        copy.start()

    barrier = pltpu.get_barrier_semaphore()

    def greet(device):
        pl.semaphore_signal(barrier, inc=1, device_id=device, device_id_type=MESH)

    @pl.loop(0, 16)
    def _(i):
        @pl.when(jnp.logical_not(jnp.logical_and(on_diagonal, i == s)))
        def _():
            greet((i, s))

    @pl.loop(1, 16)
    def _(i):
        greet(plane(i))

    @pl.loop(1, 8)
    def _(i):
        greet(along_z(i))

    greet(other_core)

    for copy in early:
        copy.wait()

    first = jnp.where(s == 0, 1.0, 0.0)
    block = jnp.concatenate(
        [
            w_in[...].astype(F32),
            prompt[...].astype(F32),
            time_vec[...].astype(F32).reshape(1, 96) * first,
            jnp.ones((1, 96), F32),
            w_out[...].astype(F32),
            gain[...].astype(F32).reshape(1, 96),
            jnp.zeros((3, 96), F32),
        ],
        axis=0,
    )
    piece[...] = jnp.concatenate([block, jnp.zeros((16, 32), F32)], axis=1).astype(BF16)

    @pl.when(on_diagonal)
    def _():
        tables[s] = piece[...]

    pl.semaphore_wait(barrier, 39 - jnp.where(on_diagonal, 1, 0))

    def to_features(i):
        return remote(piece, tables.at[s], send_p, recv_p, (m, i))

    @pl.loop(0, 16)
    def _(i):
        @pl.when(jnp.logical_not(jnp.logical_and(on_diagonal, i == m)))
        def _():
            to_features(i).start()

    in_conv.wait()
    w_tok[...] = jnp.zeros(w_tok.shape, BF16)
    for row in range(2):
        for col in range(2):
            for src_row in range(2):
                for tap in range(3):
                    offset = col + tap - 1 + 2
                    to = (offset // 2) * 64 + (2 * src_row + offset % 2) * 16
                    at = (2 * row + col) * VC
                    w_tok[to : to + 16, at : at + VC] = conv_in[src_row - row + 1, tap]

    for copy in later + [in_noise, in_steps] + last:
        copy.wait()
    noise_t[0] = noise_a[...].T
    for k in range(STEPS):
        noise_t[1 + k] = noise_b[k].T

    @pl.when(on_diagonal)
    def _():
        drain(tables.at[pl.ds(0, 15)], recv_p)

    @pl.when(jnp.logical_not(on_diagonal))
    def _():
        drain(tables, recv_p)

    want = iota((256, 256), 0)
    have = iota((256, 256), 1)
    prompt_row, out_row = want - 64, want - 96
    source = jnp.where(
        want < 64,
        (want >> 2) * 16 + (want & 3),
        jnp.where(
            want < 96,
            (prompt_row >> 1) * 16 + 4 + (prompt_row & 1),
            jnp.where(
                want < 160,
                (out_row >> 2) * 16 + 8 + (out_row & 3),
                jnp.where(want == TIME_ROW, 6, jnp.where(want == ONES_ROW, 7, jnp.where(want == GAIN_ROW, 12, -1))),
            ),
        ),
    )
    table = dot(onehot(source == have), tables[...].reshape(256, 128))
    table16 = table.astype(BF16)
    scaled_high, scaled_low = split(table * table[GAIN_ROW : GAIN_ROW + 1])
    up_part = dot(scaled_high[:, :96], w_up[...]) + dot(scaled_low[:, :96], w_up[...])
    down_part = dot(table16[96:160, :96], w_down[...])
    gram[...] = dot_t(table16, table16)
    for third in range(3):
        lanes = slice(128 * third, 128 * third + 128)
        for group in range(10):
            number = third * 10 + group
            to = (number % 2) * 16
            if group < 6:
                part[number // 2, to : to + 16] = up_part[16 * group : 16 * group + 16, lanes]
            else:
                part[number // 2, to : to + 16] = down_part[16 * group - 96 : 16 * group - 80, lanes]
    part[15, 0:32] = jnp.zeros((32, 128), F32)
    for third in range(3):
        lanes = slice(128 * third, 128 * third + 128)
        part[15, third : third + 1] = up_part[TIME_ROW : TIME_ROW + 1, lanes]
    gain_up = jnp.concatenate(
        [up_part[ONES_ROW : ONES_ROW + 1, 128 * third : 128 * third + 128] for third in range(3)], axis=0
    )
    sums = gram[ONES_ROW : ONES_ROW + 1]
    for owner in range(16):
        first_row = 8 * owner + (64 if owner >= 12 else 0)
        own = gram[pl.ds(first_row + z, 1)]
        part[owner, 32:40] = jnp.concatenate(
            [sums[:, :128], sums[:, 128:], gain_up, own[:, :128], own[:, 128:], jnp.zeros((1, 128), F32)], axis=0
        )

    def to_owner(i):
        target = lax.rem(s + i, 16)
        return remote(part.at[target], parts.at[s], send_r, recv_r, (target, m))

    @pl.loop(1, 16)
    def _(i):
        to_owner(i).start()

    parts[s] = part[s]
    drain(parts.at[pl.ds(0, 15)], recv_r)

    total = parts[0]
    for source_s in range(1, 16):
        total = total + parts[source_s]
    mean = jnp.concatenate([total[32:33], total[33:34]], axis=1) / D
    gain_rows = total[34:37]
    lane16 = iota((16, 256), 1)
    row16 = iota((16, 256), 0)
    mean_time = jnp.sum(jnp.where(iota((1, 256), 1) == TIME_ROW, mean, 0.0), axis=1, keepdims=True)
    for half in range(2):
        number = 2 * s + half
        third = lax.div(number, 10)
        group = lax.rem(number, 10)
        block = total[16 * half : 16 * half + 16]
        column = jnp.sum(jnp.where(lane16 == row16 + 16 * group, mean, 0.0), axis=1, keepdims=True)
        column = jnp.where(group < 6, column, 0.0)
        row = jnp.where(third == 0, gain_rows[0:1], jnp.where(third == 1, gain_rows[1:2], gain_rows[2:3]))
        if half == 0:
            time_rows = jnp.concatenate([mean_time * gain_rows, jnp.zeros((13, 128), F32)], axis=0)
        else:
            time_rows = jnp.zeros((16, 128), F32)
        taken = jnp.where(s == 15, time_rows, column * row)
        chunks[c, z, s, 16 * half : 16 * half + 16] = (block - taken).astype(BF16)
    own = jnp.concatenate([total[37:38], total[38:39]], axis=1)
    own_index = 8 * s + z
    own_lane = own_index + jnp.where(own_index >= 96, 64, 0)
    lane1 = iota((1, 256), 1)
    own_mean = jnp.sum(jnp.where(lane1 == own_lane, mean, 0.0), axis=1, keepdims=True)
    is_gram = jnp.logical_or(lane1 < 96, lane1 == TIME_ROW)
    own = jnp.where(is_gram, own / D - own_mean * mean, own)
    gy_own[...] = jnp.concatenate([own[:, :128], own[:, 128:], jnp.zeros((6, 128), F32)], axis=0)
    gy_z[z] = gy_own[...]

    def chunk_z(i):
        block = chunks.at[c, z, s]
        return remote(block, block, send_z, recv_z.at[i], along_z(i))

    def gram_z(i):
        return remote(gy_own, gy_z.at[z], send_g, recv_g, along_z(i))

    for i in Z_ORDER:
        gram_z(i).start()
        chunk_z(i).start()

    def from_z(i):
        return lax.rem(z + 8 - i, 8)

    def spread(i):
        block = chunks.at[c, from_z(i), s]

        @pl.loop(1, 16)
        def _(k):
            remote(block, block, send_c, recv_c.at[i], plane(k)).start()

    def to_core(i):
        block = chunks.at[c, from_z(i)]
        return remote(block, block, send_f, recv_f.at[i], other_core)

    def gram_plane(k):
        return remote(gy_all.at[s], gy_all.at[s], send_h, recv_h, plane(k))

    order = (0,) + Z_ORDER
    for n, i in enumerate(order):
        if n:
            chunk_z(i).wait_recv()
        if n == 7:
            drain(gy_z.at[pl.ds(0, 7)], recv_g)
            gy_all[s] = jnp.concatenate(
                [jnp.concatenate([gy_z[j, row : row + 1] for j in range(8)], axis=0) for row in range(2)], axis=1
            )

            @pl.loop(1, 16)
            def _(k):
                gram_plane(k).start()

        spread(i)

    own_half = pl.ds(pl.multiple_of(lax.rem(z, 2) * 64, 64), 64)
    zero_half = jnp.zeros((64, 64), F32)
    state[...] = jnp.concatenate([noise_t[0, own_half], zero_half], axis=1)
    which = assign[z]
    lane = iota((64, 128), 1)
    chosen = jnp.where(lane == 64 + which, 1.0, 0.0)

    def before_layer(now):
        latent = state[...]
        rows = latent.astype(BF16).astype(F32) + chosen
        rows_time = (rows + jnp.where(lane == 96, now, 0.0)).astype(BF16)
        mixed = dot(rows_time, gy_halves[0]) + dot(rows_time, gy_halves[1])
        second = jnp.where(lane == TIME_ROW - 128, now, 0.0)
        variance = jnp.sum(mixed[:, :128] * rows + mixed[:, 128:] * second, axis=1, keepdims=True)
        inv = lax.rsqrt(jnp.maximum(variance, 0.0) + EPSILON)
        return latent, rows.astype(BF16), inv, mixed[:, 96:160]

    def layer(core, group, rows16, inv, now):
        weights = [chunks[core, from_z(i)].reshape(512, 128) for i in group]
        up = jnp.concatenate([w[160 * t : 160 * t + 128] for w in weights for t in range(3)], axis=1)
        down = jnp.concatenate([w[160 * t + 96 : 160 * t + 160] for w in weights for t in range(3)], axis=1)
        timed = [w[480:496].astype(F32) for w in weights]
        bias = jnp.concatenate([w[t : t + 1] for w in timed for t in range(3)], axis=1) * now
        hidden = (dot(rows16, up) + bias) * inv
        return dot_t(jax.nn.gelu(hidden, approximate=True).astype(BF16), down)

    def after_layer(k, latent, moved, skip):
        change = jnp.concatenate([moved + skip, zero_half], axis=1)
        fresh = jnp.concatenate([noise_t[1 + k, own_half], zero_half], axis=1)
        state[...] = latent - STEP * change + NOISE_GAIN * fresh

    groups = (order[:4], order[4:])

    def arrived(group):
        for i in group:
            drain(chunks.at[c, 0, pl.ds(0, 15)], recv_c.at[i])
            to_core(i).start()

    arrived(groups[0])
    drain(gy_all.at[pl.ds(0, 15)], recv_h)
    gy_high, gy_low = split(gy_all[...].reshape(128, 256))
    gy_halves[0] = gy_high
    gy_halves[1] = gy_low
    latent, rows16, inv, skip = before_layer(1.0)
    moved = layer(c, groups[0], rows16, inv, 1.0)
    arrived(groups[1])
    moved = moved + layer(c, groups[1], rows16, inv, 1.0)
    vel_out[...] = jnp.concatenate([moved, moved], axis=1).astype(BF16)
    swap = remote(vel_out, vel_in, send_v, recv_v, other_core)
    swap.start()
    swap.wait_recv()
    after_layer(0, latent, (vel_out[...].astype(F32) + vel_in[...].astype(F32))[:, :64], skip)
    for i in order:
        drain(chunks.at[c, 0], recv_f.at[i])

    @pl.loop(1, STEPS)
    def _(k):
        now = 1.0 - k.astype(F32) * STEP
        latent, rows16, inv, skip = before_layer(now)
        half = [layer(core, groups[0], rows16, inv, now) + layer(core, groups[1], rows16, inv, now) for core in range(2)]
        after_layer(k, latent, half[0] + half[1], skip)

    latent = state[...][:, :64]
    image = (latent * LATENT_SCALE).astype(BF16)
    image32 = image.astype(F32)
    empty = jnp.zeros((1, 64), F32)
    before = jnp.concatenate([empty, image32[:63]], axis=0)
    after = jnp.concatenate([image32[1:], empty], axis=0)
    wide = jnp.concatenate([before, image32, after], axis=1).astype(BF16)
    conv = dot(wide, w_tok[...])
    sums4 = jnp.sum(conv, axis=0, keepdims=True)
    channel_mean = sum(sums4[:, VC * i : VC * i + VC] for i in range(4)) / 256.0
    away = conv - jnp.concatenate([channel_mean] * 4, axis=1)
    squares4 = jnp.sum(away * away, axis=0, keepdims=True)
    channel_var = sum(squares4[:, VC * i : VC * i + VC] for i in range(4)) / 256.0
    stack = jnp.concatenate(
        [channel_mean, channel_var, channel_mean * channel_mean, jnp.zeros((5, VC), F32)], axis=0
    )
    member = jnp.where((iota((VC, 128), 0) >> 4) == (iota((VC, 128), 1) & 31), 1.0, 0.0)
    grouped = dot(stack, member, precision=HIGH) / 16.0
    average = grouped[0:1]
    variance = grouped[1:2] + jnp.maximum(grouped[2:3] - average * average, 0.0)
    inv = lax.rsqrt(variance + EPSILON)
    mean_high, mean_low = split(average)
    inv_high, inv_low = split(inv)
    lane1 = iota((1, 128), 1)
    stats = jnp.where(
        lane1 < 32,
        mean_high.astype(F32),
        jnp.where(lane1 < 64, mean_low.astype(F32), jnp.where(lane1 < 96, inv_high.astype(F32), inv_low.astype(F32))),
    )
    pair, token = iota((64, 64), 0), iota((64, 64), 1)
    pairs = jnp.concatenate(
        [dot(onehot(token == 2 * pair - 1), image), dot(onehot(token == 2 * pair), image)], axis=1
    ).astype(BF16)
    row, col = iota((64, 64), 0), iota((64, 64), 1)
    place = row & 7
    wanted = jnp.logical_and(place < 3, col == 4 * (row >> 3) + 2 * c + place)
    sent = dot(onehot(wanted), pairs) + jnp.where((iota((64, 128), 0) & 7) == 3, stats, 0.0)
    tile_out[...] = sent.reshape(8, 8, 128)
    tile_z[z] = tile_out[z]

    def tile_to(i):
        to = lax.rem(z + i, 8)
        return remote(tile_out.at[to], tile_z.at[z], send_t, recv_t, (s, to * 2 + c))

    for i in Z_ORDER:
        tile_to(i).start()
    lat_out[...] = jnp.concatenate([latent[:32], latent[32:]], axis=1)
    lat_in[z] = lat_out[...]

    def latent_to(i):
        return remote(lat_out, lat_in.at[z], send_l, recv_l, along_z(i))

    for i in Z_ORDER:
        latent_to(i).start()
    drain(tile_z.at[pl.ds(0, 7)], recv_t)
    row, col = iota((32, 64), 0), iota((32, 64), 1)
    tile_pack[...] = dot(
        onehot(col == 8 * (row >> 2) + (row & 3)), tile_z[...].reshape(64, 128).astype(BF16)
    ).astype(BF16)
    tiles[s] = tile_pack[...]

    def tile_plane(k):
        return remote(tile_pack, tiles.at[s], send_u, recv_u, plane(k))

    @pl.loop(1, 16)
    def _(k):
        tile_plane(k).start()

    spread = onehot((iota((128, 512), 1) >> 2) == iota((128, 512), 0))
    slots = jnp.broadcast_to(slot_map[...].astype(F32).reshape(1, 128), (8, 128)).astype(BF16)
    slot_of = dot(slots, spread)[0:1]
    row, col = iota((64, 512), 0), iota((64, 512), 1)
    here = (16 * s + (row & 15)).astype(F32)
    pick = onehot(jnp.logical_and(slot_of == here, (col & 3) == (row >> 4)))
    in_mid.wait()
    drain(tiles.at[pl.ds(0, 15)], recv_u)
    picked = dot(pick, tiles[...].reshape(512, 128))
    tokens = jnp.concatenate(
        [picked[16 * (i // 2) : 16 * (i // 2) + 16, 64 * (i % 2) : 64 * (i % 2) + 64] for i in range(6)], axis=0
    )
    none = jnp.zeros((16, 64), F32)
    wide = jnp.concatenate(
        [jnp.concatenate([none, tokens[:80]], axis=0), tokens, jnp.concatenate([tokens[16:], none], axis=0)], axis=1
    ).astype(BF16)
    conv = dot(wide, w_tok[...])
    line, channel = iota((128, 1024), 0), iota((128, 1024), 1)
    widen = onehot(
        jnp.logical_and((line & 31) == ((channel & 511) >> 4), (line >= 64) == (channel >= 512))
    )
    wide_stats = dot(picked[48:64].astype(BF16), widen)
    average, inv = wide_stats[:, :VC], wide_stats[:, VC:]
    strength = inv * gn_gain[...].reshape(1, VC)
    left = jnp.where(m == 0, 0.0, 1.0)
    right = jnp.where(m == 15, 0.0, 1.0)
    for row, act in ((0, act0), (1, act1)):
        for at in range(10):
            token, half = (at + 1) // 2, (at + 1) % 2
            here = VC * (2 * row + half)
            shaped = (conv[16 * token : 16 * token + 16, here : here + VC] - average) * strength
            value = jax.nn.silu(shaped)
            if at == 0:
                value = value * left
            if at == 9:
                value = value * right
            act[16 * at : 16 * at + 16] = value.astype(BF16)
    ordering = onehot(
        iota((128, 128), 1) == (iota((128, 128), 0) & 7) * 16 + (iota((128, 128), 0) >> 3)
    )
    for row in range(2):
        total = jnp.concatenate(
            [
                conv[16 * (1 + at // 2) : 16 * (1 + at // 2) + 16, VC * (2 * row + at % 2) : VC * (2 * row + at % 2) + VC]
                for at in range(8)
            ],
            axis=0,
        )
        for tap in range(3):
            total = total + dot(act0[16 * tap : 16 * tap + 128], w_mid[1 - row, tap])
            total = total + dot(act1[16 * tap : 16 * tap + 128], w_mid[2 - row, tap])
        ordered = dot(ordering, total.astype(BF16)).astype(BF16)
        dec_ref[:, row] = ordered.reshape(16, 8, VC)

    drain(lat_in.at[pl.ds(0, 7)], recv_l)
    for i in range(4):
        both = jnp.concatenate(
            [half for pack in (lat_in[2 * i], lat_in[2 * i + 1]) for half in (pack[:, :64], pack[:, 64:])], axis=0
        )
        lat_ref[:, 128 * i : 128 * i + 128] = both.T

    @pl.loop(0, 16)
    def _(i):
        @pl.when(jnp.logical_not(jnp.logical_and(on_diagonal, i == m)))
        def _():
            to_features(i).wait_send()

    drain(parts.at[pl.ds(0, 15)], send_r)
    drain(chunks.at[c, 0, pl.ds(0, 7)], send_z)
    drain(gy_z.at[pl.ds(0, 7)], send_g)
    for _ in range(8):
        drain(chunks.at[c, 0, pl.ds(0, 15)], send_c)
        drain(chunks.at[c, 0], send_f)
    drain(gy_all.at[pl.ds(0, 15)], send_h)
    swap.wait_send()
    drain(tile_z.at[pl.ds(0, 7)], send_t)
    drain(lat_in.at[pl.ds(0, 7)], send_l)
    drain(tiles.at[pl.ds(0, 15)], send_u)


def per_device(*args):
    vmem, anywhere = pl.BlockSpec(memory_space=pltpu.VMEM), pl.BlockSpec(memory_space=pl.ANY)
    noise0, noise_k, assign, slot_map, prompt, time_vec, w_in, gain, w_up, w_down, w_out, conv_in, gn_gain, conv_mid = args
    dma = pltpu.SemaphoreType.DMA
    latents, decoded = pl.pallas_call(
        kernel,
        out_shape=(jax.ShapeDtypeStruct((64, 512), F32), jax.ShapeDtypeStruct((16, 2, 8, VC), BF16)),
        in_specs=[anywhere] * 14,
        out_specs=(vmem, vmem),
        scratch_shapes=[
            pltpu.SMEM((8,), jnp.int32),
            pltpu.VMEM((128,), jnp.int32),
            pltpu.VMEM((2, 96), BF16),
            pltpu.VMEM((96,), BF16),
            pltpu.VMEM((4, 96), BF16),
            pltpu.VMEM((96,), BF16),
            pltpu.VMEM((96, 384), BF16),
            pltpu.VMEM((96, 384), BF16),
            pltpu.VMEM((4, 96), BF16),
            pltpu.VMEM((3, 3, 16, VC), BF16),
            pltpu.VMEM((VC,), F32),
            pltpu.VMEM((16, 128), BF16),
            pltpu.VMEM((16, 16, 128), BF16),
            pltpu.VMEM((256, 256), F32),
            pltpu.VMEM((16, 40, 128), F32),
            pltpu.VMEM((16, 40, 128), F32),
            pltpu.VMEM((2, 8, 16, 32, 128), BF16),
            pltpu.VMEM((8, 128), F32),
            pltpu.VMEM((8, 8, 128), F32),
            pltpu.VMEM((16, 8, 256), F32),
            pltpu.VMEM((2, 128, 256), BF16),
            pltpu.VMEM((64, 128), BF16),
            pltpu.VMEM((64, 128), BF16),
            pltpu.VMEM((64, 128), F32),
            pltpu.VMEM((8, 8, 128), F32),
            pltpu.VMEM((8, 8, 128), F32),
            pltpu.VMEM((32, 128), BF16),
            pltpu.VMEM((16, 32, 128), BF16),
            pltpu.VMEM((32, 128), F32),
            pltpu.VMEM((8, 32, 128), F32),
            pltpu.VMEM((64, 128), F32),
            pltpu.VMEM((STEPS, 64, 128), F32),
            pltpu.VMEM((1 + STEPS, 128, 64), F32),
            pltpu.VMEM((3, 3, VC, VC), BF16),
            pltpu.VMEM((192, 4 * VC), BF16),
            pltpu.VMEM((160, VC), BF16),
            pltpu.VMEM((160, VC), BF16),
            dma((14,)),
            dma, dma,
            dma, dma,
            dma, dma((8,)),
            dma, dma,
            dma, dma((8,)),
            dma, dma((8,)),
            dma, dma,
            dma, dma,
            dma, dma,
            dma, dma,
            dma, dma,
        ],
        compiler_params=pltpu.CompilerParams(collective_id=0, has_side_effects=True, vmem_limit_bytes=62 << 20),
        name="rollout",
    )(
        assign, slot_map, noise0.T, noise_k.transpose(0, 2, 1), prompt, time_vec, w_in, gain, w_up, w_down.T, w_out.T,
        conv_in, gn_gain, conv_mid,
    )
    return latents.T, decoded


def solution(mesh):
    return jax.shard_map(
        per_device,
        mesh=mesh,
        in_specs=(
            P("segment", None),
            P(None, "segment", None),
            P("segment"),
            P(),
            P("segment", "mp"),
            P("mp"),
            P("segment", "mp"),
            P("mp"),
            P("segment", "mp"),
            P("mp", "segment"),
            P("mp", "segment"),
            P(),
            P(),
            P(),
        ),
        out_specs=(P("segment", None), P("segment", None, "mp", None)),
        check_vma=False,
    )
```

```python
import jax
import jax.numpy as jnp
from jax import lax
from jax.experimental import pallas as pl
from jax.experimental.pallas import tpu as pltpu
from jax.sharding import PartitionSpec as P

MESH = pl.DeviceIdType.MESH
F32, BF16 = jnp.float32, jnp.bfloat16
HIGH = lax.Precision.HIGHEST
D, FF, VC, GROUPS, STEPS = 1536, 6144, 512, 32, 4
EPSILON = 1e-6
LATENT_SCALE = 1.0 / 1.5305
STEP = 1.0 / STEPS
NOISE_GAIN = 0.5 * STEP**0.5
TIME_ROW, ONES_ROW, GAIN_ROW = 160, 161, 162
Z_ORDER = (1, 7, 2, 6, 3, 5, 4)


def dot(a, b, **kw):
    return jnp.dot(a, b, preferred_element_type=F32, **kw)


def dot_t(a, b):
    return lax.dot_general(a, b, (((1,), (1,)), ((), ())), preferred_element_type=F32)


def iota(shape, dim):
    return lax.broadcasted_iota(jnp.int32, shape, dim)


def onehot(mask):
    return jnp.where(mask, 1.0, 0.0).astype(BF16)


def split(value):
    high = value.astype(BF16)
    return high, (value - high.astype(F32)).astype(BF16)


def kernel(
    assign_in, slot_in, noise0, noise_k, prompt_in, time_in, w_in_in, gain_in, w_up_in, w_down_in, w_out_in, conv_in_in,
    gn_in, conv_mid,
    lat_ref, dec_ref,
    assign, slot_map, prompt, time_vec, w_in, gain, w_up, w_down, w_out, conv_in, gn_gain,
    piece, tables, gram, part, parts, chunks, gy_own, gy_z, gy_all, gy_halves, vel_out, vel_in, state,
    tile_out, tile_z, tile_pack, tiles, lat_out, lat_in, noise_a, noise_b, noise_t, w_mid, w_tok, act0, act1,
    in_sem, send_p, recv_p, send_r, recv_r, send_z, recv_z, send_g, recv_g, send_c, recv_c, send_f, recv_f, send_h, recv_h, send_v, recv_v,
    send_t, recv_t, send_u, recv_u, send_l, recv_l,
):
    s, m = lax.axis_index("segment"), lax.axis_index("mp")
    z, c = lax.div(m, 2), lax.rem(m, 2)
    on_diagonal = m == s

    def remote(src, dst, ssem, rsem, device):
        return pltpu.make_async_remote_copy(
            src_ref=src, dst_ref=dst, send_sem=ssem, recv_sem=rsem, device_id=device, device_id_type=MESH
        )

    def plane(i):
        return lax.rem(s + i, 16), m

    def along_z(i):
        return s, lax.rem(z + i, 8) * 2 + c

    other_core = (s, m + 1 - 2 * c)

    def drain(ref, sem):
        pltpu.make_async_copy(ref, ref, sem).wait()

    barrier = pltpu.get_barrier_semaphore()

    def greet(device):
        pl.semaphore_signal(barrier, inc=1, device_id=device, device_id_type=MESH)

    @pl.loop(0, 16)
    def _(i):
        @pl.when(jnp.logical_not(jnp.logical_and(on_diagonal, i == s)))
        def _():
            greet((i, s))

    @pl.loop(1, 16)
    def _(i):
        greet(plane(i))

    @pl.loop(1, 8)
    def _(i):
        greet(along_z(i))

    greet(other_core)

    lanes = pl.ds(pl.multiple_of(lax.div(z, 2) * 128, 128), 128)
    early = [
        pltpu.make_async_copy(src, dst, in_sem.at[3 + n])
        for n, (src, dst) in enumerate(
            [(w_in_in, w_in), (prompt_in, prompt), (time_in, time_vec), (gain_in, gain), (w_out_in, w_out)]
        )
    ]
    in_conv = pltpu.make_async_copy(conv_in_in, conv_in, in_sem.at[8])
    later = [
        pltpu.make_async_copy(src, dst, in_sem.at[9 + n])
        for n, (src, dst) in enumerate([(w_up_in, w_up), (w_down_in, w_down)])
    ]
    last = [
        pltpu.make_async_copy(src, dst, in_sem.at[11 + n])
        for n, (src, dst) in enumerate([(assign_in, assign), (slot_in, slot_map), (gn_in, gn_gain)])
    ]
    in_noise = pltpu.make_async_copy(noise0.at[:, lanes], noise_a, in_sem.at[0])
    in_steps = pltpu.make_async_copy(noise_k.at[:, :, lanes], noise_b, in_sem.at[1])
    in_mid = pltpu.make_async_copy(conv_mid, w_mid, in_sem.at[2])
    for copy in early + later + [in_conv, in_noise, in_steps] + last + [in_mid]:
        copy.start()

    for copy in early:
        copy.wait()

    first = jnp.where(s == 0, 1.0, 0.0)
    block = jnp.concatenate(
        [
            w_in[...].astype(F32),
            prompt[...].astype(F32),
            time_vec[...].astype(F32).reshape(1, 96) * first,
            jnp.ones((1, 96), F32),
            w_out[...].astype(F32),
            gain[...].astype(F32).reshape(1, 96),
            jnp.zeros((3, 96), F32),
        ],
        axis=0,
    )
    piece[...] = jnp.concatenate([block, jnp.zeros((16, 32), F32)], axis=1).astype(BF16)

    @pl.when(on_diagonal)
    def _():
        tables[s] = piece[...]

    pl.semaphore_wait(barrier, 39 - jnp.where(on_diagonal, 1, 0))

    def to_features(i):
        return remote(piece, tables.at[s], send_p, recv_p, (m, i))

    @pl.loop(0, 16)
    def _(i):
        @pl.when(jnp.logical_not(jnp.logical_and(on_diagonal, i == m)))
        def _():
            to_features(i).start()

    in_conv.wait()
    w_tok[...] = jnp.zeros(w_tok.shape, BF16)
    for row in range(2):
        for col in range(2):
            for src_row in range(2):
                for tap in range(3):
                    offset = col + tap - 1 + 2
                    to = (offset // 2) * 64 + (2 * src_row + offset % 2) * 16
                    at = (2 * row + col) * VC
                    w_tok[to : to + 16, at : at + VC] = conv_in[src_row - row + 1, tap]

    for copy in later + [in_noise, in_steps] + last:
        copy.wait()
    noise_t[0] = noise_a[...].T
    for k in range(STEPS):
        noise_t[1 + k] = noise_b[k].T

    @pl.when(on_diagonal)
    def _():
        drain(tables.at[pl.ds(0, 15)], recv_p)

    @pl.when(jnp.logical_not(on_diagonal))
    def _():
        drain(tables, recv_p)

    want = iota((256, 256), 0)
    have = iota((256, 256), 1)
    prompt_row, out_row = want - 64, want - 96
    source = jnp.where(
        want < 64,
        (want >> 2) * 16 + (want & 3),
        jnp.where(
            want < 96,
            (prompt_row >> 1) * 16 + 4 + (prompt_row & 1),
            jnp.where(
                want < 160,
                (out_row >> 2) * 16 + 8 + (out_row & 3),
                jnp.where(want == TIME_ROW, 6, jnp.where(want == ONES_ROW, 7, jnp.where(want == GAIN_ROW, 12, -1))),
            ),
        ),
    )
    table = dot(onehot(source == have), tables[...].reshape(256, 128))
    table16 = table.astype(BF16)
    scaled_high, scaled_low = split(table * table[GAIN_ROW : GAIN_ROW + 1])
    up_part = dot(scaled_high[:, :96], w_up[...]) + dot(scaled_low[:, :96], w_up[...])
    down_part = dot(table16[96:160, :96], w_down[...])
    gram[...] = dot_t(table16, table16)
    for third in range(3):
        lanes = slice(128 * third, 128 * third + 128)
        for group in range(10):
            number = third * 10 + group
            to = (number % 2) * 16
            if group < 6:
                part[number // 2, to : to + 16] = up_part[16 * group : 16 * group + 16, lanes]
            else:
                part[number // 2, to : to + 16] = down_part[16 * group - 96 : 16 * group - 80, lanes]
    part[15, 0:32] = jnp.zeros((32, 128), F32)
    for third in range(3):
        lanes = slice(128 * third, 128 * third + 128)
        part[15, third : third + 1] = up_part[TIME_ROW : TIME_ROW + 1, lanes]
    gain_up = jnp.concatenate(
        [up_part[ONES_ROW : ONES_ROW + 1, 128 * third : 128 * third + 128] for third in range(3)], axis=0
    )
    sums = gram[ONES_ROW : ONES_ROW + 1]
    for owner in range(16):
        first_row = 8 * owner + (64 if owner >= 12 else 0)
        own = gram[pl.ds(first_row + z, 1)]
        part[owner, 32:40] = jnp.concatenate(
            [sums[:, :128], sums[:, 128:], gain_up, own[:, :128], own[:, 128:], jnp.zeros((1, 128), F32)], axis=0
        )

    def to_owner(i):
        target = lax.rem(s + i, 16)
        return remote(part.at[target], parts.at[s], send_r, recv_r, (target, m))

    @pl.loop(1, 16)
    def _(i):
        to_owner(i).start()

    parts[s] = part[s]
    drain(parts.at[pl.ds(0, 15)], recv_r)

    total = parts[0]
    for source_s in range(1, 16):
        total = total + parts[source_s]
    mean = jnp.concatenate([total[32:33], total[33:34]], axis=1) / D
    gain_rows = total[34:37]
    lane16 = iota((16, 256), 1)
    row16 = iota((16, 256), 0)
    mean_time = jnp.sum(jnp.where(iota((1, 256), 1) == TIME_ROW, mean, 0.0), axis=1, keepdims=True)
    for half in range(2):
        number = 2 * s + half
        third = lax.div(number, 10)
        group = lax.rem(number, 10)
        block = total[16 * half : 16 * half + 16]
        column = jnp.sum(jnp.where(lane16 == row16 + 16 * group, mean, 0.0), axis=1, keepdims=True)
        column = jnp.where(group < 6, column, 0.0)
        row = jnp.where(third == 0, gain_rows[0:1], jnp.where(third == 1, gain_rows[1:2], gain_rows[2:3]))
        if half == 0:
            time_rows = jnp.concatenate([mean_time * gain_rows, jnp.zeros((13, 128), F32)], axis=0)
        else:
            time_rows = jnp.zeros((16, 128), F32)
        taken = jnp.where(s == 15, time_rows, column * row)
        chunks[c, z, s, 16 * half : 16 * half + 16] = (block - taken).astype(BF16)
    own = jnp.concatenate([total[37:38], total[38:39]], axis=1)
    own_index = 8 * s + z
    own_lane = own_index + jnp.where(own_index >= 96, 64, 0)
    lane1 = iota((1, 256), 1)
    own_mean = jnp.sum(jnp.where(lane1 == own_lane, mean, 0.0), axis=1, keepdims=True)
    is_gram = jnp.logical_or(lane1 < 96, lane1 == TIME_ROW)
    own = jnp.where(is_gram, own / D - own_mean * mean, own)
    gy_own[...] = jnp.concatenate([own[:, :128], own[:, 128:], jnp.zeros((6, 128), F32)], axis=0)
    gy_z[z] = gy_own[...]

    def chunk_z(i):
        block = chunks.at[c, z, s]
        return remote(block, block, send_z, recv_z.at[i], along_z(i))

    def gram_z(i):
        return remote(gy_own, gy_z.at[z], send_g, recv_g, along_z(i))

    for i in Z_ORDER:
        gram_z(i).start()
        chunk_z(i).start()

    def from_z(i):
        return lax.rem(z + 8 - i, 8)

    def spread(i):
        block = chunks.at[c, from_z(i), s]

        @pl.loop(1, 16)
        def _(k):
            remote(block, block, send_c, recv_c.at[i], plane(k)).start()

    def to_core(i):
        block = chunks.at[c, from_z(i)]
        return remote(block, block, send_f, recv_f.at[i], other_core)

    def gram_plane(k):
        return remote(gy_all.at[s], gy_all.at[s], send_h, recv_h, plane(k))

    order = (0,) + Z_ORDER
    for n, i in enumerate(order):
        if n:
            chunk_z(i).wait_recv()
        if n == 7:
            drain(gy_z.at[pl.ds(0, 7)], recv_g)
            gy_all[s] = jnp.concatenate(
                [jnp.concatenate([gy_z[j, row : row + 1] for j in range(8)], axis=0) for row in range(2)], axis=1
            )

            @pl.loop(1, 16)
            def _(k):
                gram_plane(k).start()

        spread(i)

    own_half = pl.ds(pl.multiple_of(lax.rem(z, 2) * 64, 64), 64)
    zero_half = jnp.zeros((64, 64), F32)
    state[...] = jnp.concatenate([noise_t[0, own_half], zero_half], axis=1)
    which = assign[z]
    lane = iota((64, 128), 1)
    chosen = jnp.where(lane == 64 + which, 1.0, 0.0)

    def before_layer(now):
        latent = state[...]
        rows = latent.astype(BF16).astype(F32) + chosen
        rows_time = (rows + jnp.where(lane == 96, now, 0.0)).astype(BF16)
        mixed = dot(rows_time, gy_halves[0]) + dot(rows_time, gy_halves[1])
        second = jnp.where(lane == TIME_ROW - 128, now, 0.0)
        variance = jnp.sum(mixed[:, :128] * rows + mixed[:, 128:] * second, axis=1, keepdims=True)
        inv = lax.rsqrt(jnp.maximum(variance, 0.0) + EPSILON)
        return latent, rows.astype(BF16), inv, mixed[:, 96:160]

    def layer(core, group, rows16, inv, now):
        weights = [chunks[core, from_z(i)].reshape(512, 128) for i in group]
        up = jnp.concatenate([w[160 * t : 160 * t + 128] for w in weights for t in range(3)], axis=1)
        down = jnp.concatenate([w[160 * t + 96 : 160 * t + 160] for w in weights for t in range(3)], axis=1)
        timed = [w[480:496].astype(F32) for w in weights]
        bias = jnp.concatenate([w[t : t + 1] for w in timed for t in range(3)], axis=1) * now
        hidden = (dot(rows16, up) + bias) * inv
        return dot_t(jax.nn.gelu(hidden, approximate=True).astype(BF16), down)

    def after_layer(k, latent, moved, skip):
        change = jnp.concatenate([moved + skip, zero_half], axis=1)
        fresh = jnp.concatenate([noise_t[1 + k, own_half], zero_half], axis=1)
        state[...] = latent - STEP * change + NOISE_GAIN * fresh

    groups = (order[:4], order[4:])

    def arrived(group):
        for i in group:
            drain(chunks.at[c, 0, pl.ds(0, 15)], recv_c.at[i])
            to_core(i).start()

    arrived(groups[0])
    drain(gy_all.at[pl.ds(0, 15)], recv_h)
    gy_high, gy_low = split(gy_all[...].reshape(128, 256))
    gy_halves[0] = gy_high
    gy_halves[1] = gy_low
    latent, rows16, inv, skip = before_layer(1.0)
    moved = layer(c, groups[0], rows16, inv, 1.0)
    arrived(groups[1])
    moved = moved + layer(c, groups[1], rows16, inv, 1.0)
    vel_out[...] = jnp.concatenate([moved, moved], axis=1).astype(BF16)
    swap = remote(vel_out, vel_in, send_v, recv_v, other_core)
    swap.start()
    swap.wait_recv()
    after_layer(0, latent, (vel_out[...].astype(F32) + vel_in[...].astype(F32))[:, :64], skip)
    for i in order:
        drain(chunks.at[c, 0], recv_f.at[i])

    @pl.loop(1, STEPS)
    def _(k):
        now = 1.0 - k.astype(F32) * STEP
        latent, rows16, inv, skip = before_layer(now)
        half = [layer(core, groups[0], rows16, inv, now) + layer(core, groups[1], rows16, inv, now) for core in range(2)]
        after_layer(k, latent, half[0] + half[1], skip)

    latent = state[...][:, :64]
    image = (latent * LATENT_SCALE).astype(BF16)
    image32 = image.astype(F32)
    empty = jnp.zeros((1, 64), F32)
    before = jnp.concatenate([empty, image32[:63]], axis=0)
    after = jnp.concatenate([image32[1:], empty], axis=0)
    wide = jnp.concatenate([before, image32, after], axis=1).astype(BF16)
    conv = dot(wide, w_tok[...])
    sums4 = jnp.sum(conv, axis=0, keepdims=True)
    channel_mean = sum(sums4[:, VC * i : VC * i + VC] for i in range(4)) / 256.0
    away = conv - jnp.concatenate([channel_mean] * 4, axis=1)
    squares4 = jnp.sum(away * away, axis=0, keepdims=True)
    channel_var = sum(squares4[:, VC * i : VC * i + VC] for i in range(4)) / 256.0
    stack = jnp.concatenate(
        [channel_mean, channel_var, channel_mean * channel_mean, jnp.zeros((5, VC), F32)], axis=0
    )
    member = jnp.where((iota((VC, 128), 0) >> 4) == (iota((VC, 128), 1) & 31), 1.0, 0.0)
    grouped = dot(stack, member, precision=HIGH) / 16.0
    average = grouped[0:1]
    variance = grouped[1:2] + jnp.maximum(grouped[2:3] - average * average, 0.0)
    inv = lax.rsqrt(variance + EPSILON)
    mean_high, mean_low = split(average)
    inv_high, inv_low = split(inv)
    lane1 = iota((1, 128), 1)
    stats = jnp.where(
        lane1 < 32,
        mean_high.astype(F32),
        jnp.where(lane1 < 64, mean_low.astype(F32), jnp.where(lane1 < 96, inv_high.astype(F32), inv_low.astype(F32))),
    )
    pair, token = iota((64, 64), 0), iota((64, 64), 1)
    pairs = jnp.concatenate(
        [dot(onehot(token == 2 * pair - 1), image), dot(onehot(token == 2 * pair), image)], axis=1
    ).astype(BF16)
    row, col = iota((64, 64), 0), iota((64, 64), 1)
    place = row & 7
    wanted = jnp.logical_and(place < 3, col == 4 * (row >> 3) + 2 * c + place)
    sent = dot(onehot(wanted), pairs) + jnp.where((iota((64, 128), 0) & 7) == 3, stats, 0.0)
    tile_out[...] = sent.reshape(8, 8, 128)
    tile_z[z] = tile_out[z]

    def tile_to(i):
        to = lax.rem(z + i, 8)
        return remote(tile_out.at[to], tile_z.at[z], send_t, recv_t, (s, to * 2 + c))

    for i in Z_ORDER:
        tile_to(i).start()
    lat_out[...] = jnp.concatenate([latent[:32], latent[32:]], axis=1)
    lat_in[z] = lat_out[...]

    def latent_to(i):
        return remote(lat_out, lat_in.at[z], send_l, recv_l, along_z(i))

    for i in Z_ORDER:
        latent_to(i).start()
    drain(tile_z.at[pl.ds(0, 7)], recv_t)
    row, col = iota((32, 64), 0), iota((32, 64), 1)
    tile_pack[...] = dot(
        onehot(col == 8 * (row >> 2) + (row & 3)), tile_z[...].reshape(64, 128).astype(BF16)
    ).astype(BF16)
    tiles[s] = tile_pack[...]

    def tile_plane(k):
        return remote(tile_pack, tiles.at[s], send_u, recv_u, plane(k))

    @pl.loop(1, 16)
    def _(k):
        tile_plane(k).start()

    spread = onehot((iota((128, 512), 1) >> 2) == iota((128, 512), 0))
    slots = jnp.broadcast_to(slot_map[...].astype(F32).reshape(1, 128), (8, 128)).astype(BF16)
    slot_of = dot(slots, spread)[0:1]
    row, col = iota((64, 512), 0), iota((64, 512), 1)
    here = (16 * s + (row & 15)).astype(F32)
    pick = onehot(jnp.logical_and(slot_of == here, (col & 3) == (row >> 4)))
    drain(lat_in.at[pl.ds(0, 7)], recv_l)
    for i in range(4):
        both = jnp.concatenate(
            [half for pack in (lat_in[2 * i], lat_in[2 * i + 1]) for half in (pack[:, :64], pack[:, 64:])], axis=0
        )
        lat_ref[:, 128 * i : 128 * i + 128] = both.T
    in_mid.wait()
    drain(tiles.at[pl.ds(0, 15)], recv_u)
    picked = dot(pick, tiles[...].reshape(512, 128))
    tokens = jnp.concatenate(
        [picked[16 * (i // 2) : 16 * (i // 2) + 16, 64 * (i % 2) : 64 * (i % 2) + 64] for i in range(6)], axis=0
    )
    none = jnp.zeros((16, 64), F32)
    wide = jnp.concatenate(
        [jnp.concatenate([none, tokens[:80]], axis=0), tokens, jnp.concatenate([tokens[16:], none], axis=0)], axis=1
    ).astype(BF16)
    conv = dot(wide, w_tok[...])
    line, channel = iota((128, 1024), 0), iota((128, 1024), 1)
    widen = onehot(
        jnp.logical_and((line & 31) == ((channel & 511) >> 4), (line >= 64) == (channel >= 512))
    )
    wide_stats = dot(picked[48:64].astype(BF16), widen)
    average, inv = wide_stats[:, :VC], wide_stats[:, VC:]
    strength = inv * gn_gain[...].reshape(1, VC)
    left = jnp.where(m == 0, 0.0, 1.0)
    right = jnp.where(m == 15, 0.0, 1.0)
    for row, act in ((0, act0), (1, act1)):
        for at in range(10):
            token, half = (at + 1) // 2, (at + 1) % 2
            here = VC * (2 * row + half)
            shaped = (conv[16 * token : 16 * token + 16, here : here + VC] - average) * strength
            value = jax.nn.silu(shaped)
            if at == 0:
                value = value * left
            if at == 9:
                value = value * right
            act[16 * at : 16 * at + 16] = value.astype(BF16)
    ordering = onehot(
        iota((128, 128), 1) == (iota((128, 128), 0) & 7) * 16 + (iota((128, 128), 0) >> 3)
    )
    for row in range(2):
        total = jnp.concatenate(
            [
                conv[16 * (1 + at // 2) : 16 * (1 + at // 2) + 16, VC * (2 * row + at % 2) : VC * (2 * row + at % 2) + VC]
                for at in range(8)
            ],
            axis=0,
        )
        for tap in range(3):
            total = total + dot(act0[16 * tap : 16 * tap + 128], w_mid[1 - row, tap])
            total = total + dot(act1[16 * tap : 16 * tap + 128], w_mid[2 - row, tap])
        ordered = dot(ordering, total.astype(BF16)).astype(BF16)
        dec_ref[:, row] = ordered.reshape(16, 8, VC)

    @pl.loop(0, 16)
    def _(i):
        @pl.when(jnp.logical_not(jnp.logical_and(on_diagonal, i == m)))
        def _():
            to_features(i).wait_send()

    drain(parts.at[pl.ds(0, 15)], send_r)
    drain(chunks.at[c, 0, pl.ds(0, 7)], send_z)
    drain(gy_z.at[pl.ds(0, 7)], send_g)
    for _ in range(8):
        drain(chunks.at[c, 0, pl.ds(0, 15)], send_c)
        drain(chunks.at[c, 0], send_f)
    drain(gy_all.at[pl.ds(0, 15)], send_h)
    swap.wait_send()
    drain(tile_z.at[pl.ds(0, 7)], send_t)
    drain(lat_in.at[pl.ds(0, 7)], send_l)
    drain(tiles.at[pl.ds(0, 15)], send_u)


def per_device(*args):
    vmem, anywhere = pl.BlockSpec(memory_space=pltpu.VMEM), pl.BlockSpec(memory_space=pl.ANY)
    noise0, noise_k, assign, slot_map, prompt, time_vec, w_in, gain, w_up, w_down, w_out, conv_in, gn_gain, conv_mid = args
    dma = pltpu.SemaphoreType.DMA
    latents, decoded = pl.pallas_call(
        kernel,
        out_shape=(pltpu.VMEM((64, 512), F32), pltpu.VMEM((16, 2, 8, VC), BF16)),
        in_specs=[anywhere] * 14,
        out_specs=(vmem, vmem),
        scratch_shapes=[
            pltpu.SMEM((8,), jnp.int32),
            pltpu.VMEM((128,), jnp.int32),
            pltpu.VMEM((2, 96), BF16),
            pltpu.VMEM((96,), BF16),
            pltpu.VMEM((4, 96), BF16),
            pltpu.VMEM((96,), BF16),
            pltpu.VMEM((96, 384), BF16),
            pltpu.VMEM((96, 384), BF16),
            pltpu.VMEM((4, 96), BF16),
            pltpu.VMEM((3, 3, 16, VC), BF16),
            pltpu.VMEM((VC,), F32),
            pltpu.VMEM((16, 128), BF16),
            pltpu.VMEM((16, 16, 128), BF16),
            pltpu.VMEM((256, 256), F32),
            pltpu.VMEM((16, 40, 128), F32),
            pltpu.VMEM((16, 40, 128), F32),
            pltpu.VMEM((2, 8, 16, 32, 128), BF16),
            pltpu.VMEM((8, 128), F32),
            pltpu.VMEM((8, 8, 128), F32),
            pltpu.VMEM((16, 8, 256), F32),
            pltpu.VMEM((2, 128, 256), BF16),
            pltpu.VMEM((64, 128), BF16),
            pltpu.VMEM((64, 128), BF16),
            pltpu.VMEM((64, 128), F32),
            pltpu.VMEM((8, 8, 128), F32),
            pltpu.VMEM((8, 8, 128), F32),
            pltpu.VMEM((32, 128), BF16),
            pltpu.VMEM((16, 32, 128), BF16),
            pltpu.VMEM((32, 128), F32),
            pltpu.VMEM((8, 32, 128), F32),
            pltpu.VMEM((64, 128), F32),
            pltpu.VMEM((STEPS, 64, 128), F32),
            pltpu.VMEM((1 + STEPS, 128, 64), F32),
            pltpu.VMEM((3, 3, VC, VC), BF16),
            pltpu.VMEM((192, 4 * VC), BF16),
            pltpu.VMEM((160, VC), BF16),
            pltpu.VMEM((160, VC), BF16),
            dma((14,)),
            dma, dma,
            dma, dma,
            dma, dma((8,)),
            dma, dma,
            dma, dma((8,)),
            dma, dma((8,)),
            dma, dma,
            dma, dma,
            dma, dma,
            dma, dma,
            dma, dma,
        ],
        compiler_params=pltpu.CompilerParams(collective_id=0, has_side_effects=True, vmem_limit_bytes=62 << 20),
        name="rollout",
    )(
        assign, slot_map, noise0.T, noise_k.transpose(0, 2, 1), prompt, time_vec, w_in, gain, w_up, w_down.T, w_out.T,
        conv_in, gn_gain, conv_mid,
    )
    return latents.T, decoded


def solution(mesh):
    return jax.shard_map(
        per_device,
        mesh=mesh,
        in_specs=(
            P("segment", None),
            P(None, "segment", None),
            P("segment"),
            P(),
            P("segment", "mp"),
            P("mp"),
            P("segment", "mp"),
            P("mp"),
            P("segment", "mp"),
            P("mp", "segment"),
            P("mp", "segment"),
            P(),
            P(),
            P(),
        ),
        out_specs=(P("segment", None), P("segment", None, "mp", None)),
        check_vma=False,
    )
```

```python
import jax
import jax.numpy as jnp
from jax import lax
from jax.experimental import pallas as pl
from jax.experimental.pallas import tpu as pltpu
from jax.sharding import PartitionSpec as P

MESH = pl.DeviceIdType.MESH
F32, BF16 = jnp.float32, jnp.bfloat16
HIGH = lax.Precision.HIGHEST
D, FF, VC, GROUPS, STEPS = 1536, 6144, 512, 32, 4
EPSILON = 1e-6
LATENT_SCALE = 1.0 / 1.5305
STEP = 1.0 / STEPS
NOISE_GAIN = 0.5 * STEP**0.5
TIME_ROW, ONES_ROW, GAIN_ROW = 160, 161, 162
Z_ORDER = (1, 7, 2, 6, 3, 5, 4)


def dot(a, b, **kw):
    return jnp.dot(a, b, preferred_element_type=F32, **kw)


def dot_t(a, b):
    return lax.dot_general(a, b, (((1,), (1,)), ((), ())), preferred_element_type=F32)


def iota(shape, dim):
    return lax.broadcasted_iota(jnp.int32, shape, dim)


def onehot(mask):
    return jnp.where(mask, 1.0, 0.0).astype(BF16)


def split(value):
    high = value.astype(BF16)
    return high, (value - high.astype(F32)).astype(BF16)


def kernel(
    assign_in, slot_in, noise0, noise_k, prompt_in, time_in, w_in_in, gain_in, w_up_in, w_down_in, w_out_in, conv_in_in,
    gn_in, conv_mid,
    lat_ref, dec_ref,
    assign, slot_map, prompt, time_vec, w_in, gain, w_up, w_down, w_out, conv_in, gn_gain,
    piece, tables, gram, part, parts, chunks, gy_own, gy_z, gy_all, gy_halves, vel_out, vel_in, state,
    tile_out, tile_z, tile_pack, tiles, lat_out, lat_in, noise_a, noise_b, noise_t, w_mid, w_tok, acts,
    in_sem, send_p, recv_p, send_r, recv_r, send_z, recv_z, send_g, recv_g, send_c, recv_c, send_f, recv_f, send_h, recv_h, send_v, recv_v,
    send_t, recv_t, send_u, recv_u, send_l, recv_l,
):
    s, m = lax.axis_index("segment"), lax.axis_index("mp")
    z, c = lax.div(m, 2), lax.rem(m, 2)
    on_diagonal = m == s

    def remote(src, dst, ssem, rsem, device):
        return pltpu.make_async_remote_copy(
            src_ref=src, dst_ref=dst, send_sem=ssem, recv_sem=rsem, device_id=device, device_id_type=MESH
        )

    def plane(i):
        return lax.rem(s + i, 16), m

    def along_z(i):
        return s, lax.rem(z + i, 8) * 2 + c

    other_core = (s, m + 1 - 2 * c)

    def drain(ref, sem):
        pltpu.make_async_copy(ref, ref, sem).wait()

    barrier = pltpu.get_barrier_semaphore()

    def greet(device):
        pl.semaphore_signal(barrier, inc=1, device_id=device, device_id_type=MESH)

    @pl.loop(0, 16)
    def _(i):
        @pl.when(jnp.logical_not(jnp.logical_and(on_diagonal, i == s)))
        def _():
            greet((i, s))

    @pl.loop(1, 16)
    def _(i):
        greet(plane(i))

    @pl.loop(1, 8)
    def _(i):
        greet(along_z(i))

    greet(other_core)

    lanes = pl.ds(pl.multiple_of(lax.div(z, 2) * 128, 128), 128)
    early = [
        pltpu.make_async_copy(src, dst, in_sem.at[3 + n])
        for n, (src, dst) in enumerate(
            [(w_in_in, w_in), (prompt_in, prompt), (time_in, time_vec), (gain_in, gain), (w_out_in, w_out)]
        )
    ]
    in_conv = pltpu.make_async_copy(conv_in_in, conv_in, in_sem.at[8])
    later = [
        pltpu.make_async_copy(src, dst, in_sem.at[9 + n])
        for n, (src, dst) in enumerate([(w_up_in, w_up), (w_down_in, w_down)])
    ]
    last = [
        pltpu.make_async_copy(src, dst, in_sem.at[11 + n])
        for n, (src, dst) in enumerate([(assign_in, assign), (slot_in, slot_map), (gn_in, gn_gain)])
    ]
    in_noise = pltpu.make_async_copy(noise0.at[:, lanes], noise_a, in_sem.at[0])
    in_steps = pltpu.make_async_copy(noise_k.at[:, :, lanes], noise_b, in_sem.at[1])
    in_mid = pltpu.make_async_copy(conv_mid, w_mid, in_sem.at[2])
    for copy in early + later + [in_conv, in_noise, in_steps] + last + [in_mid]:
        copy.start()

    for copy in early:
        copy.wait()

    first = jnp.where(s == 0, 1.0, 0.0)
    block = jnp.concatenate(
        [
            w_in[...].astype(F32),
            prompt[...].astype(F32),
            time_vec[...].astype(F32).reshape(1, 96) * first,
            jnp.ones((1, 96), F32),
            w_out[...].astype(F32),
            gain[...].astype(F32).reshape(1, 96),
            jnp.zeros((3, 96), F32),
        ],
        axis=0,
    )
    piece[...] = jnp.concatenate([block, jnp.zeros((16, 32), F32)], axis=1).astype(BF16)

    @pl.when(on_diagonal)
    def _():
        tables[s] = piece[...]

    pl.semaphore_wait(barrier, 39 - jnp.where(on_diagonal, 1, 0))

    def to_features(i):
        return remote(piece, tables.at[s], send_p, recv_p, (m, i))

    @pl.loop(0, 16)
    def _(i):
        @pl.when(jnp.logical_not(jnp.logical_and(on_diagonal, i == m)))
        def _():
            to_features(i).start()

    in_conv.wait()
    w_tok[...] = jnp.zeros(w_tok.shape, BF16)
    for row in range(2):
        for col in range(2):
            for src_row in range(2):
                for tap in range(3):
                    offset = col + tap - 1 + 2
                    to = (offset // 2) * 64 + (2 * src_row + offset % 2) * 16
                    at = (2 * row + col) * VC
                    w_tok[to : to + 16, at : at + VC] = conv_in[src_row - row + 1, tap]

    for copy in later + [in_noise, in_steps] + last:
        copy.wait()
    noise_t[0] = noise_a[...].T
    for k in range(STEPS):
        noise_t[1 + k] = noise_b[k].T

    @pl.when(on_diagonal)
    def _():
        drain(tables.at[pl.ds(0, 15)], recv_p)

    @pl.when(jnp.logical_not(on_diagonal))
    def _():
        drain(tables, recv_p)

    want = iota((256, 256), 0)
    have = iota((256, 256), 1)
    prompt_row, out_row = want - 64, want - 96
    source = jnp.where(
        want < 64,
        (want >> 2) * 16 + (want & 3),
        jnp.where(
            want < 96,
            (prompt_row >> 1) * 16 + 4 + (prompt_row & 1),
            jnp.where(
                want < 160,
                (out_row >> 2) * 16 + 8 + (out_row & 3),
                jnp.where(want == TIME_ROW, 6, jnp.where(want == ONES_ROW, 7, jnp.where(want == GAIN_ROW, 12, -1))),
            ),
        ),
    )
    table = dot(onehot(source == have), tables[...].reshape(256, 128))
    table16 = table.astype(BF16)
    scaled_high, scaled_low = split(table * table[GAIN_ROW : GAIN_ROW + 1])
    up_part = dot(scaled_high[:, :96], w_up[...]) + dot(scaled_low[:, :96], w_up[...])
    down_part = dot(table16[96:160, :96], w_down[...])
    gram[...] = dot_t(table16, table16)
    for third in range(3):
        lanes = slice(128 * third, 128 * third + 128)
        for group in range(10):
            number = third * 10 + group
            to = (number % 2) * 16
            if group < 6:
                part[number // 2, to : to + 16] = up_part[16 * group : 16 * group + 16, lanes]
            else:
                part[number // 2, to : to + 16] = down_part[16 * group - 96 : 16 * group - 80, lanes]
    part[15, 0:32] = jnp.zeros((32, 128), F32)
    for third in range(3):
        lanes = slice(128 * third, 128 * third + 128)
        part[15, third : third + 1] = up_part[TIME_ROW : TIME_ROW + 1, lanes]
    gain_up = jnp.concatenate(
        [up_part[ONES_ROW : ONES_ROW + 1, 128 * third : 128 * third + 128] for third in range(3)], axis=0
    )
    sums = gram[ONES_ROW : ONES_ROW + 1]
    for owner in range(16):
        first_row = 8 * owner + (64 if owner >= 12 else 0)
        own = gram[pl.ds(first_row + z, 1)]
        part[owner, 32:40] = jnp.concatenate(
            [sums[:, :128], sums[:, 128:], gain_up, own[:, :128], own[:, 128:], jnp.zeros((1, 128), F32)], axis=0
        )

    def to_owner(i):
        target = lax.rem(s + i, 16)
        return remote(part.at[target], parts.at[s], send_r, recv_r, (target, m))

    @pl.loop(1, 16)
    def _(i):
        to_owner(i).start()

    parts[s] = part[s]
    drain(parts.at[pl.ds(0, 15)], recv_r)

    total = parts[0]
    for source_s in range(1, 16):
        total = total + parts[source_s]
    mean = jnp.concatenate([total[32:33], total[33:34]], axis=1) / D
    gain_rows = total[34:37]
    lane16 = iota((16, 256), 1)
    row16 = iota((16, 256), 0)
    mean_time = jnp.sum(jnp.where(iota((1, 256), 1) == TIME_ROW, mean, 0.0), axis=1, keepdims=True)
    for half in range(2):
        number = 2 * s + half
        third = lax.div(number, 10)
        group = lax.rem(number, 10)
        block = total[16 * half : 16 * half + 16]
        column = jnp.sum(jnp.where(lane16 == row16 + 16 * group, mean, 0.0), axis=1, keepdims=True)
        column = jnp.where(group < 6, column, 0.0)
        row = jnp.where(third == 0, gain_rows[0:1], jnp.where(third == 1, gain_rows[1:2], gain_rows[2:3]))
        if half == 0:
            time_rows = jnp.concatenate([mean_time * gain_rows, jnp.zeros((13, 128), F32)], axis=0)
        else:
            time_rows = jnp.zeros((16, 128), F32)
        taken = jnp.where(s == 15, time_rows, column * row)
        chunks[c, z, s, 16 * half : 16 * half + 16] = (block - taken).astype(BF16)
    own = jnp.concatenate([total[37:38], total[38:39]], axis=1)
    own_index = 8 * s + z
    own_lane = own_index + jnp.where(own_index >= 96, 64, 0)
    lane1 = iota((1, 256), 1)
    own_mean = jnp.sum(jnp.where(lane1 == own_lane, mean, 0.0), axis=1, keepdims=True)
    is_gram = jnp.logical_or(lane1 < 96, lane1 == TIME_ROW)
    own = jnp.where(is_gram, own / D - own_mean * mean, own)
    gy_own[...] = jnp.concatenate([own[:, :128], own[:, 128:], jnp.zeros((6, 128), F32)], axis=0)
    gy_z[z] = gy_own[...]

    def chunk_z(i):
        block = chunks.at[c, z, s]
        return remote(block, block, send_z, recv_z.at[i], along_z(i))

    def gram_z(i):
        return remote(gy_own, gy_z.at[z], send_g, recv_g, along_z(i))

    for i in Z_ORDER:
        gram_z(i).start()
        chunk_z(i).start()

    def from_z(i):
        return lax.rem(z + 8 - i, 8)

    def spread(i):
        block = chunks.at[c, from_z(i), s]

        @pl.loop(1, 16)
        def _(k):
            remote(block, block, send_c, recv_c.at[i], plane(k)).start()

    def to_core(i):
        block = chunks.at[c, from_z(i)]
        return remote(block, block, send_f, recv_f.at[i], other_core)

    def gram_plane(k):
        return remote(gy_all.at[s], gy_all.at[s], send_h, recv_h, plane(k))

    order = (0,) + Z_ORDER
    for n, i in enumerate(order):
        if n:
            chunk_z(i).wait_recv()
        if n == 7:
            drain(gy_z.at[pl.ds(0, 7)], recv_g)
            gy_all[s] = jnp.concatenate(
                [jnp.concatenate([gy_z[j, row : row + 1] for j in range(8)], axis=0) for row in range(2)], axis=1
            )

            @pl.loop(1, 16)
            def _(k):
                gram_plane(k).start()

        spread(i)

    own_half = pl.ds(pl.multiple_of(lax.rem(z, 2) * 64, 64), 64)
    zero_half = jnp.zeros((64, 64), F32)
    state[...] = jnp.concatenate([noise_t[0, own_half], zero_half], axis=1)
    which = assign[z]
    lane = iota((64, 128), 1)
    chosen = jnp.where(lane == 64 + which, 1.0, 0.0)

    def before_layer(now):
        latent = state[...]
        rows = latent.astype(BF16).astype(F32) + chosen
        rows_time = (rows + jnp.where(lane == 96, now, 0.0)).astype(BF16)
        mixed = dot(jnp.concatenate([rows_time, rows_time], axis=1), gy_halves[...].reshape(256, 256))
        second = jnp.where(lane == TIME_ROW - 128, now, 0.0)
        variance = jnp.sum(mixed[:, :128] * rows + mixed[:, 128:] * second, axis=1, keepdims=True)
        inv = lax.rsqrt(jnp.maximum(variance, 0.0) + EPSILON)
        return latent, rows.astype(BF16), inv, mixed[:, 96:160]

    def layer(core, group, rows16, inv, now):
        weights = [chunks[core, from_z(i)].reshape(512, 128) for i in group]
        up = jnp.concatenate([w[160 * t : 160 * t + 128] for w in weights for t in range(3)], axis=1)
        down = jnp.concatenate([w[160 * t + 96 : 160 * t + 160] for w in weights for t in range(3)], axis=1)
        timed = [w[480:496].astype(F32) for w in weights]
        bias = jnp.concatenate([w[t : t + 1] for w in timed for t in range(3)], axis=1) * now
        hidden = (dot(rows16, up) + bias) * inv
        return dot_t(jax.nn.gelu(hidden, approximate=True).astype(BF16), down)

    def after_layer(k, latent, moved, skip):
        change = jnp.concatenate([moved + skip, zero_half], axis=1)
        fresh = jnp.concatenate([noise_t[1 + k, own_half], zero_half], axis=1)
        state[...] = latent - STEP * change + NOISE_GAIN * fresh

    groups = (order[:4], order[4:])

    def arrived(group):
        for i in group:
            drain(chunks.at[c, 0, pl.ds(0, 15)], recv_c.at[i])
            to_core(i).start()

    arrived(groups[0])
    drain(gy_all.at[pl.ds(0, 15)], recv_h)
    gy_high, gy_low = split(gy_all[...].reshape(128, 256))
    gy_halves[0] = gy_high
    gy_halves[1] = gy_low
    latent, rows16, inv, skip = before_layer(1.0)
    moved = layer(c, groups[0], rows16, inv, 1.0)
    arrived(groups[1])
    moved = moved + layer(c, groups[1], rows16, inv, 1.0)
    vel_out[...] = jnp.concatenate([moved, moved], axis=1).astype(BF16)
    swap = remote(vel_out, vel_in, send_v, recv_v, other_core)
    swap.start()
    swap.wait_recv()
    after_layer(0, latent, (vel_out[...].astype(F32) + vel_in[...].astype(F32))[:, :64], skip)
    for i in order:
        drain(chunks.at[c, 0], recv_f.at[i])

    @pl.loop(1, STEPS)
    def _(k):
        now = 1.0 - k.astype(F32) * STEP
        latent, rows16, inv, skip = before_layer(now)
        half = [layer(core, groups[0], rows16, inv, now) + layer(core, groups[1], rows16, inv, now) for core in range(2)]
        after_layer(k, latent, half[0] + half[1], skip)

    latent = state[...][:, :64]
    image = (latent * LATENT_SCALE).astype(BF16)
    image32 = image.astype(F32)
    empty = jnp.zeros((1, 64), F32)
    before = jnp.concatenate([empty, image32[:63]], axis=0)
    after = jnp.concatenate([image32[1:], empty], axis=0)
    wide = jnp.concatenate([before, image32, after], axis=1).astype(BF16)
    conv = dot(wide, w_tok[...])
    sums4 = jnp.sum(conv, axis=0, keepdims=True)
    channel_mean = sum(sums4[:, VC * i : VC * i + VC] for i in range(4)) / 256.0
    away = conv - jnp.concatenate([channel_mean] * 4, axis=1)
    squares4 = jnp.sum(away * away, axis=0, keepdims=True)
    channel_var = sum(squares4[:, VC * i : VC * i + VC] for i in range(4)) / 256.0
    stack = jnp.concatenate(
        [channel_mean, channel_var, channel_mean * channel_mean, jnp.zeros((5, VC), F32)], axis=0
    )
    member = jnp.where((iota((VC, 128), 0) >> 4) == (iota((VC, 128), 1) & 31), 1.0, 0.0)
    grouped = dot(stack, member, precision=HIGH) / 16.0
    average = grouped[0:1]
    variance = grouped[1:2] + jnp.maximum(grouped[2:3] - average * average, 0.0)
    inv = lax.rsqrt(variance + EPSILON)
    mean_high, mean_low = split(average)
    inv_high, inv_low = split(inv)
    lane1 = iota((1, 128), 1)
    stats = jnp.where(
        lane1 < 32,
        mean_high.astype(F32),
        jnp.where(lane1 < 64, mean_low.astype(F32), jnp.where(lane1 < 96, inv_high.astype(F32), inv_low.astype(F32))),
    )
    pair, token = iota((64, 64), 0), iota((64, 64), 1)
    pairs = jnp.concatenate(
        [dot(onehot(token == 2 * pair - 1), image), dot(onehot(token == 2 * pair), image)], axis=1
    ).astype(BF16)
    row, col = iota((64, 64), 0), iota((64, 64), 1)
    place = row & 7
    wanted = jnp.logical_and(place < 3, col == 4 * (row >> 3) + 2 * c + place)
    sent = dot(onehot(wanted), pairs) + jnp.where((iota((64, 128), 0) & 7) == 3, stats, 0.0)
    tile_out[...] = sent.reshape(8, 8, 128)
    tile_z[z] = tile_out[z]

    def tile_to(i):
        to = lax.rem(z + i, 8)
        return remote(tile_out.at[to], tile_z.at[z], send_t, recv_t, (s, to * 2 + c))

    for i in Z_ORDER:
        tile_to(i).start()
    lat_out[...] = jnp.concatenate([latent[:32], latent[32:]], axis=1)
    lat_in[z] = lat_out[...]

    def latent_to(i):
        return remote(lat_out, lat_in.at[z], send_l, recv_l, along_z(i))

    for i in Z_ORDER:
        latent_to(i).start()
    drain(tile_z.at[pl.ds(0, 7)], recv_t)
    row, col = iota((32, 64), 0), iota((32, 64), 1)
    tile_pack[...] = dot(
        onehot(col == 8 * (row >> 2) + (row & 3)), tile_z[...].reshape(64, 128).astype(BF16)
    ).astype(BF16)
    tiles[s] = tile_pack[...]

    def tile_plane(k):
        return remote(tile_pack, tiles.at[s], send_u, recv_u, plane(k))

    @pl.loop(1, 16)
    def _(k):
        tile_plane(k).start()

    spread = onehot((iota((128, 512), 1) >> 2) == iota((128, 512), 0))
    slots = jnp.broadcast_to(slot_map[...].astype(F32).reshape(1, 128), (8, 128)).astype(BF16)
    slot_of = dot(slots, spread)[0:1]
    row, col = iota((64, 512), 0), iota((64, 512), 1)
    here = (16 * s + (row & 15)).astype(F32)
    pick = onehot(jnp.logical_and(slot_of == here, (col & 3) == (row >> 4)))
    drain(lat_in.at[pl.ds(0, 7)], recv_l)
    for i in range(4):
        both = jnp.concatenate(
            [half for pack in (lat_in[2 * i], lat_in[2 * i + 1]) for half in (pack[:, :64], pack[:, 64:])], axis=0
        )
        lat_ref[:, 128 * i : 128 * i + 128] = both.T
    in_mid.wait()
    drain(tiles.at[pl.ds(0, 15)], recv_u)
    picked = dot(pick, tiles[...].reshape(512, 128))
    tokens = jnp.concatenate(
        [picked[16 * (i // 2) : 16 * (i // 2) + 16, 64 * (i % 2) : 64 * (i % 2) + 64] for i in range(6)], axis=0
    )
    none = jnp.zeros((16, 64), F32)
    wide = jnp.concatenate(
        [jnp.concatenate([none, tokens[:80]], axis=0), tokens, jnp.concatenate([tokens[16:], none], axis=0)], axis=1
    ).astype(BF16)
    conv = dot(wide, w_tok[...])
    line, channel = iota((128, 1024), 0), iota((128, 1024), 1)
    widen = onehot(
        jnp.logical_and((line & 31) == ((channel & 511) >> 4), (line >= 64) == (channel >= 512))
    )
    wide_stats = dot(picked[48:64].astype(BF16), widen)
    average, inv = wide_stats[:, :VC], wide_stats[:, VC:]
    strength = inv * gn_gain[...].reshape(1, VC)
    left = jnp.where(m == 0, 0.0, 1.0)
    right = jnp.where(m == 15, 0.0, 1.0)
    for row in range(2):
        for at in range(10):
            token, half = (at + 1) // 2, (at + 1) % 2
            here = VC * (2 * row + half)
            shaped = (conv[16 * token : 16 * token + 16, here : here + VC] - average) * strength
            value = jax.nn.silu(shaped)
            if at == 0:
                value = value * left
            if at == 9:
                value = value * right
            acts[row, 16 * at : 16 * at + 16] = value.astype(BF16)
    ordering = onehot(
        iota((128, 128), 1) == (iota((128, 128), 0) & 7) * 16 + (iota((128, 128), 0) >> 3)
    )
    same_row = sum(dot(acts[:, 16 * tap : 16 * tap + 128].reshape(256, VC), w_mid[1, tap]) for tap in range(3))
    for row in range(2):
        total = jnp.concatenate(
            [
                conv[16 * (1 + at // 2) : 16 * (1 + at // 2) + 16, VC * (2 * row + at % 2) : VC * (2 * row + at % 2) + VC]
                for at in range(8)
            ],
            axis=0,
        )
        total = total + same_row[128 * row : 128 * row + 128]
        for tap in range(3):
            total = total + dot(acts[1 - row, 16 * tap : 16 * tap + 128], w_mid[2 - 2 * row, tap])
        ordered = dot(ordering, total.astype(BF16)).astype(BF16)
        dec_ref[:, row] = ordered.reshape(16, 8, VC)

    @pl.loop(0, 16)
    def _(i):
        @pl.when(jnp.logical_not(jnp.logical_and(on_diagonal, i == m)))
        def _():
            to_features(i).wait_send()

    drain(parts.at[pl.ds(0, 15)], send_r)
    drain(chunks.at[c, 0, pl.ds(0, 7)], send_z)
    drain(gy_z.at[pl.ds(0, 7)], send_g)
    for _ in range(8):
        drain(chunks.at[c, 0, pl.ds(0, 15)], send_c)
        drain(chunks.at[c, 0], send_f)
    drain(gy_all.at[pl.ds(0, 15)], send_h)
    swap.wait_send()
    drain(tile_z.at[pl.ds(0, 7)], send_t)
    drain(lat_in.at[pl.ds(0, 7)], send_l)
    drain(tiles.at[pl.ds(0, 15)], send_u)


def per_device(*args):
    vmem, anywhere = pl.BlockSpec(memory_space=pltpu.VMEM), pl.BlockSpec(memory_space=pl.ANY)
    noise0, noise_k, assign, slot_map, prompt, time_vec, w_in, gain, w_up, w_down, w_out, conv_in, gn_gain, conv_mid = args
    dma = pltpu.SemaphoreType.DMA
    latents, decoded = pl.pallas_call(
        kernel,
        out_shape=(pltpu.VMEM((64, 512), F32), pltpu.VMEM((16, 2, 8, VC), BF16)),
        in_specs=[anywhere] * 14,
        out_specs=(vmem, vmem),
        scratch_shapes=[
            pltpu.SMEM((8,), jnp.int32),
            pltpu.VMEM((128,), jnp.int32),
            pltpu.VMEM((2, 96), BF16),
            pltpu.VMEM((96,), BF16),
            pltpu.VMEM((4, 96), BF16),
            pltpu.VMEM((96,), BF16),
            pltpu.VMEM((96, 384), BF16),
            pltpu.VMEM((96, 384), BF16),
            pltpu.VMEM((4, 96), BF16),
            pltpu.VMEM((3, 3, 16, VC), BF16),
            pltpu.VMEM((VC,), F32),
            pltpu.VMEM((16, 128), BF16),
            pltpu.VMEM((16, 16, 128), BF16),
            pltpu.VMEM((256, 256), F32),
            pltpu.VMEM((16, 40, 128), F32),
            pltpu.VMEM((16, 40, 128), F32),
            pltpu.VMEM((2, 8, 16, 32, 128), BF16),
            pltpu.VMEM((8, 128), F32),
            pltpu.VMEM((8, 8, 128), F32),
            pltpu.VMEM((16, 8, 256), F32),
            pltpu.VMEM((2, 128, 256), BF16),
            pltpu.VMEM((64, 128), BF16),
            pltpu.VMEM((64, 128), BF16),
            pltpu.VMEM((64, 128), F32),
            pltpu.VMEM((8, 8, 128), F32),
            pltpu.VMEM((8, 8, 128), F32),
            pltpu.VMEM((32, 128), BF16),
            pltpu.VMEM((16, 32, 128), BF16),
            pltpu.VMEM((32, 128), F32),
            pltpu.VMEM((8, 32, 128), F32),
            pltpu.VMEM((64, 128), F32),
            pltpu.VMEM((STEPS, 64, 128), F32),
            pltpu.VMEM((1 + STEPS, 128, 64), F32),
            pltpu.VMEM((3, 3, VC, VC), BF16),
            pltpu.VMEM((192, 4 * VC), BF16),
            pltpu.VMEM((2, 160, VC), BF16),
            dma((14,)),
            dma, dma,
            dma, dma,
            dma, dma((8,)),
            dma, dma,
            dma, dma((8,)),
            dma, dma((8,)),
            dma, dma,
            dma, dma,
            dma, dma,
            dma, dma,
            dma, dma,
        ],
        compiler_params=pltpu.CompilerParams(collective_id=0, has_side_effects=True, vmem_limit_bytes=62 << 20),
        name="rollout",
    )(
        assign, slot_map, noise0.T, noise_k.transpose(0, 2, 1), prompt, time_vec, w_in, gain, w_up, w_down.T, w_out.T,
        conv_in, gn_gain, conv_mid,
    )
    return latents.T, decoded


def solution(mesh):
    return jax.shard_map(
        per_device,
        mesh=mesh,
        in_specs=(
            P("segment", None),
            P(None, "segment", None),
            P("segment"),
            P(),
            P("segment", "mp"),
            P("mp"),
            P("segment", "mp"),
            P("mp"),
            P("segment", "mp"),
            P("mp", "segment"),
            P("mp", "segment"),
            P(),
            P(),
            P(),
        ),
        out_specs=(P("segment", None), P("segment", None, "mp", None)),
        check_vma=False,
    )
```
